32 devices in a mesh: seq: 16 (over z, y, x), head: 2 (over core).
Axes of the slice: x: 2, y: 2, z: 4, core: 2. Of those that a mesh axis runs over, the one named last changes fastest.
Arguments:
- tokens: bfloat16 [16384, 1024], P('seq'), may hold values from -6 to 6
- memory: bfloat16 [16384, 1024], P('seq'), may hold values from -6 to 6
- cotangent: bfloat16 [16384, 1024], P('seq'), may hold values from -6 to 6
- tgt_lengths: int32 [32], replicated, may hold values from 1 to 1792, as said below
- mem_lengths: int32 [32], replicated, may hold values from 1 to 1792, as said below
- self_query: bfloat16 [1024, 1024], P(None, 'head'), may hold values from -0.1875 to 0.1875
- self_key: bfloat16 [1024, 1024], P(None, 'head'), may hold values from -0.1875 to 0.1875
- self_value: bfloat16 [1024, 1024], P(None, 'head'), may hold values from -0.1875 to 0.1875
- self_output: bfloat16 [1024, 1024], P('head'), may hold values from -0.75 to 0.75
- cross_query: bfloat16 [1024, 1024], P(None, 'head'), may hold values from -0.1875 to 0.1875
- cross_key: bfloat16 [1024, 1024], P(None, 'head'), may hold values from -0.1875 to 0.1875
- cross_value: bfloat16 [1024, 1024], P(None, 'head'), may hold values from -0.1875 to 0.1875
- cross_output: bfloat16 [1024, 1024], P('head'), may hold values from -0.75 to 0.75
- hidden_in: bfloat16 [1024, 4096], P(None, 'head'), may hold values from -0.1875 to 0.1875
- hidden_out: bfloat16 [4096, 1024], P('head'), may hold values from -0.09375 to 0.09375
- prefix_keys: float32 [30, 1024], P(None, 'head'), may hold values from -6 to 6
- prefix_values: float32 [30, 1024], P(None, 'head'), may hold values from -6 to 6
- adapter_down: float32 [1024, 512], P(None, 'head'), may hold values from -0.1875 to 0.1875
- adapter_down_bias: float32 [512], P('head'), may hold values from -3 to 3
- adapter_up: float32 [512, 1024], P('head'), may hold values from -0.25 to 0.25
- adapter_up_bias: float32 [1024], replicated, may hold values from -1.2 to 1.2
Outputs:
- outputs: bfloat16 [16384, 1024], P('seq')
- grad_tokens: float32 [16384, 1024], P('seq')
- grad_memory: float32 [16384, 1024], P('seq')
- grad_prefix_keys: float32 [30, 1024], P(None, 'head')
- grad_prefix_values: float32 [30, 1024], P(None, 'head')
- grad_adapter_down: float32 [1024, 512], P(None, 'head')
- grad_adapter_down_bias: float32 [512], P('head')
- grad_adapter_up: float32 [512, 1024], P('head')
- grad_adapter_up_bias: float32 [1024], replicated
The draws below stay inside these ranges and needn't reach their ends.
Inputs may be any that keep to these rules, and one draw needn't show every extreme that they name: `tgt_lengths`: target sequences are packed in order; each holds at most 1792 tokens and one holds exactly 1792. `mem_lengths`: target sequence j reads encoder sequence j, both packed in order; where encoder sequence j ends in the packed encoder rows differs from where target sequence j ends in the packed target tokens by at most 128, and by exactly 128 for some j; each encoder sequence holds at most 1792 rows and one holds exactly 1792.
All inputs are finite; a program needn't handle non-finite values.
Results may differ from the reference program's by a relative error of at most 0.03.
Values may be sent and summed in bfloat16 or wider, within the bound.
No kernel may reach another device: no remote copies, remote signals or barrier semaphores. Data moves between devices by JAX's collectives and lax.ppermute only.
A program may use at most 768 MiB of HBM per device.

```python
import jax
import jax.numpy as jnp
from jax import lax

D = 1024
HEAD_DIM = 64
FF = 4096
ADAPT = 512
PREFIX = 30
TOK_DEV = 1024
NDOC = 32
SEQ_MAX = 1792
DRIFT = 128
TOKENS = 16384
MEM_TOKENS = 16384


def documents(key):
    parts = jax.random.split(key, 4)
    span = TOKENS // TOK_DEV
    shard = jax.random.randint(parts[0], (), 0, span - 2).astype(jnp.int32)
    offset = jax.random.randint(parts[1], (), TOK_DEV // 4 + 1, TOK_DEV - TOK_DEV // 8).astype(jnp.int32)
    start = shard * TOK_DEV + offset
    weights = jax.random.randint(parts[2], (NDOC,), 1, 4).astype(jnp.int32)
    drifts = jax.random.randint(parts[3], (NDOC,), -DRIFT, DRIFT + 1).astype(jnp.int32)
    order = jnp.arange(NDOC, dtype=jnp.int32)
    longest = jnp.clip((NDOC - 1) * start // (TOKENS - SEQ_MAX), 1, NDOC - 2).astype(jnp.int32)
    after_count = NDOC - 1 - longest
    remain = TOKENS - start - SEQ_MAX
    before = order < longest
    after = order > longest
    weight_before = jnp.where(before, weights, 0).astype(jnp.int32)
    weight_after = jnp.where(after, weights, 0).astype(jnp.int32)
    cum_before = jnp.cumsum(weight_before).astype(jnp.int32)
    cum_after = jnp.cumsum(weight_after).astype(jnp.int32)
    end_before = order + 1 + (start - longest) * cum_before // jnp.sum(weight_before)
    end_after = start + SEQ_MAX + (order - longest) + (remain - after_count) * cum_after // jnp.sum(weight_after)
    bounds = jnp.where(before, end_before, jnp.where(order == longest, start + SEQ_MAX, end_after)).astype(jnp.int32)
    drifts = jnp.where(order == longest, DRIFT, drifts)
    drifts = jnp.where(order == longest - 1, DRIFT, drifts)
    drifts = jnp.where(order == NDOC - 1, 0, drifts).astype(jnp.int32)
    lifted = lax.cummax(bounds + drifts - order, axis=0)
    mem_bounds = jnp.minimum(lifted + order, TOKENS - (NDOC - 1 - order)).astype(jnp.int32)
    zero = jnp.zeros((1,), jnp.int32)
    tgt = bounds - jnp.concatenate([zero, bounds[:-1]])
    mem = mem_bounds - jnp.concatenate([zero, mem_bounds[:-1]])
    return (tgt.astype(jnp.int32), mem.astype(jnp.int32))


def draw_tgt_lengths(key, part):
    return documents(key)[0]


def draw_mem_lengths(key, part):
    return documents(key)[1]


def level_of(stream_key, shape, cuts, low, largest):
    def one(position, blocks):
        steps = jax.random.uniform(jax.random.fold_in(jax.random.fold_in(stream_key, 6), position), (blocks,), jnp.float32, low / len(cuts), largest / len(cuts))
        return jnp.repeat(jnp.exp(steps), shape[position] // blocks).reshape((-1,) + (1,) * (len(shape) - position - 1))

    gain = one(*cuts[0])
    for cut in cuts[1:]:
        gain = gain * one(*cut)
    return gain


def scatter_about(rng, shape, scale, most, pieces=(), kind=jnp.bfloat16):
    values = jax.random.normal(rng, shape, jnp.float32) * scale
    if len(pieces) > 0:
        values = level_of(rng, shape, pieces, -0.22, 0.18) * values
    return jnp.clip(values, min=-most, max=most).astype(kind)


def setup_inputs(seed: int = 0) -> dict:
    seeds = jax.random.split(jax.random.key(seed), 22)
    return {
        "tokens": scatter_about(seeds[0], (TOKENS, D), 1.0, 6.0, ((0, 16),)),
        "memory": scatter_about(seeds[1], (MEM_TOKENS, D), 1.0, 6.0, ((0, 16),)),
        "cotangent": scatter_about(seeds[2], (TOKENS, D), 1.0, 6.0, ((0, 16),)),
        "tgt_lengths": draw_tgt_lengths(jax.random.fold_in(seeds[21], 71), 0),
        "mem_lengths": draw_mem_lengths(jax.random.fold_in(seeds[21], 71), 0),
        "self_query": scatter_about(seeds[5], (D, D), D ** -0.5, 0.1875, ((1, 2),)),
        "self_key": scatter_about(seeds[6], (D, D), D ** -0.5, 0.1875, ((1, 2),)),
        "self_value": scatter_about(seeds[7], (D, D), D ** -0.5, 0.1875, ((1, 2),)),
        "self_output": scatter_about(seeds[8], (D, D), (D // 16) ** -0.5, 0.75, ((0, 2),)),
        "cross_query": scatter_about(seeds[9], (D, D), D ** -0.5, 0.1875, ((1, 2),)),
        "cross_key": scatter_about(seeds[10], (D, D), D ** -0.5, 0.1875, ((1, 2),)),
        "cross_value": scatter_about(seeds[11], (D, D), D ** -0.5, 0.1875, ((1, 2),)),
        "cross_output": scatter_about(seeds[12], (D, D), (D // 16) ** -0.5, 0.75, ((0, 2),)),
        "hidden_in": scatter_about(seeds[13], (D, FF), D ** -0.5, 0.1875, ((1, 2),)),
        "hidden_out": scatter_about(seeds[14], (FF, D), FF ** -0.5, 0.09375, ((0, 2),)),
        "prefix_keys": scatter_about(seeds[15], (PREFIX, D), 1.0, 6.0, ((1, 2),), jnp.float32),
        "prefix_values": scatter_about(seeds[16], (PREFIX, D), 1.0, 6.0, ((1, 2),), jnp.float32),
        "adapter_down": scatter_about(seeds[17], (D, ADAPT), D ** -0.5, 0.1875, ((1, 2),), jnp.float32),
        "adapter_down_bias": scatter_about(seeds[18], (ADAPT,), 0.5, 3.0, ((0, 2),), jnp.float32),
        "adapter_up": scatter_about(seeds[19], (ADAPT, D), ADAPT ** -0.5, 0.25, ((0, 2),), jnp.float32),
        "adapter_up_bias": scatter_about(seeds[20], (D,), 0.2, 1.2, (), jnp.float32),
    }


EPS = 1e-05
MASKED = -1e+30
HIGH = lax.Precision.HIGHEST

@jax.custom_vjp
def low(v):
    return lax.optimization_barrier(v.astype(jnp.bfloat16)).astype(jnp.float32)

@jax.custom_vjp
def low_back(v):
    return v

def low_keep(v):
    return (low(v), None)

def low_pass(kept, grad):
    return (grad,)

def back_keep(v):
    return (v, None)

def back_low(kept, grad):
    return (low(grad),)
low.defvjp(low_keep, low_pass)
low_back.defvjp(back_keep, back_low)

def matmul(left, right):
    return jnp.dot(left, right, precision=HIGH)

def norm_rows(value):
    center = value - lax.optimization_barrier(jnp.mean(value, axis=-1, keepdims=True))
    spread = lax.optimization_barrier(jnp.mean(center * center, axis=-1, keepdims=True))
    return center * lax.rsqrt(spread + EPS)

def gelu_exact(value):
    return jax.nn.gelu(value, approximate=False)

def doc_ids(lengths, places):
    bounds = jnp.cumsum(lengths).astype(jnp.int32)
    return lax.optimization_barrier(jnp.sum((places[:, None] >= bounds[None, :]).astype(jnp.int32), axis=1))

def attention(query, keys, values, query_doc, key_doc, causal, prefix):
    length = query.shape[0]
    block = min(512, length)
    blocks = length // block
    heads = query.shape[1] // HEAD_DIM
    factor = HEAD_DIM ** (-0.5)
    key_place = jnp.arange(keys.shape[0], dtype=jnp.int32)

    def one_block(entry):
        head = entry // blocks
        start = (entry % blocks * block).astype(jnp.int32)
        column = (head * HEAD_DIM).astype(jnp.int32)
        query_rows = lax.dynamic_slice(query, (start, column), (block, HEAD_DIM))
        key_cols = lax.dynamic_slice_in_dim(keys, column, HEAD_DIM, 1)
        value_cols = lax.dynamic_slice_in_dim(values, column, HEAD_DIM, 1)
        places = start + jnp.arange(block, dtype=jnp.int32)
        row_doc = lax.dynamic_slice_in_dim(query_doc, start, block, 0)
        allowed = row_doc[:, None] == key_doc[None, :]
        if causal:
            allowed = allowed & (key_place[None, :] <= places[:, None])
        logits = matmul(query_rows, key_cols.T) * factor
        scores = low_back(jnp.where(allowed, logits, MASKED))
        row_max = lax.optimization_barrier(jnp.max(scores, axis=1, keepdims=True))
        if prefix is not None:
            prefix_cols = lax.dynamic_slice_in_dim(prefix[0], column, HEAD_DIM, 1)
            prefix_vals = lax.dynamic_slice_in_dim(prefix[1], column, HEAD_DIM, 1)
            prefix_scores = low_back(matmul(query_rows, prefix_cols.T) * factor)
            row_max = jnp.maximum(row_max, lax.optimization_barrier(jnp.max(prefix_scores, axis=1, keepdims=True)))
        weights = jnp.exp(scores - row_max)
        row_total = lax.optimization_barrier(jnp.sum(weights, axis=1, keepdims=True))
        if prefix is not None:
            prefix_weights = jnp.exp(prefix_scores - row_max)
            row_total = row_total + lax.optimization_barrier(jnp.sum(prefix_weights, axis=1, keepdims=True))
        result = matmul(low(weights / row_total), value_cols)
        if prefix is not None:
            result = result + matmul(low(prefix_weights / row_total), prefix_vals)
        return result
    entries = jnp.arange(heads * blocks, dtype=jnp.int32)
    results = lax.map(jax.checkpoint(one_block), entries)
    results = results.reshape(heads, blocks * block, HEAD_DIM)
    return jnp.transpose(results, (1, 0, 2)).reshape(length, heads * HEAD_DIM)

def layer(tokens, memory, prefix_keys, prefix_values, adapter_down, adapter_down_bias, adapter_up, adapter_up_bias, frozen, tok_doc, mem_doc):
    self_query, self_key, self_value, self_output, cross_query, cross_key, cross_value, cross_output, hidden_in, hidden_out = frozen

    def project(rows, weight):
        return low_back(low(matmul(rows, weight)))
    query = project(tokens, self_query)
    keys = project(tokens, self_key)
    values = project(tokens, self_value)
    prefix = (low(prefix_keys), low(prefix_values))
    attended = low_back(low(attention(query, keys, values, tok_doc, tok_doc, True, prefix)))
    first = norm_rows(tokens + low_back(matmul(attended, self_output)))
    first_low = low(first)
    cross_q = project(first_low, cross_query)
    mem_keys = project(memory, cross_key)
    mem_values = project(memory, cross_value)
    crossed = low_back(low(attention(cross_q, mem_keys, mem_values, tok_doc, mem_doc, False, None)))
    second = norm_rows(first + low_back(matmul(crossed, cross_output)))
    second_low = low(second)
    inner = low_back(matmul(second_low, hidden_in))
    gated = low(gelu_exact(inner))
    down = low_back(matmul(second_low, low(adapter_down)) + adapter_down_bias)
    adapted = low(gelu_exact(down))
    branch = low_back(matmul(gated, hidden_out) + 4.0 * (matmul(adapted, low(adapter_up)) + adapter_up_bias))
    return norm_rows(second + branch)

def reference(tokens, memory, cotangent, tgt_lengths, mem_lengths, self_query, self_key, self_value, self_output, cross_query, cross_key, cross_value, cross_output, hidden_in, hidden_out, prefix_keys, prefix_values, adapter_down, adapter_down_bias, adapter_up, adapter_up_bias):
    frozen = tuple((weight.astype(jnp.float32) for weight in (self_query, self_key, self_value, self_output, cross_query, cross_key, cross_value, cross_output, hidden_in, hidden_out)))
    tok_doc = doc_ids(tgt_lengths, jnp.arange(TOKENS, dtype=jnp.int32))
    mem_doc = doc_ids(mem_lengths, jnp.arange(MEM_TOKENS, dtype=jnp.int32))

    def forward(tok, mem, pre_k, pre_v, down_w, down_b, up_w, up_b):
        return layer(tok, mem, pre_k, pre_v, down_w, down_b, up_w, up_b, frozen, tok_doc, mem_doc)
    result, backward = jax.vjp(forward, tokens.astype(jnp.float32), memory.astype(jnp.float32), prefix_keys, prefix_values, adapter_down, adapter_down_bias, adapter_up, adapter_up_bias)
    grads = backward(cotangent.astype(jnp.float32))
    return (result.astype(jnp.bfloat16), grads[0], grads[1], grads[2], grads[3], grads[4], grads[5], grads[6], grads[7])
```

```python
import functools
from typing import NamedTuple

import jax
import jax.numpy as jnp
from jax import lax
from jax.experimental import pallas as pl
from jax.experimental.pallas import tpu as pltpu
from jax.sharding import PartitionSpec as P

HEAD_DIM = 64
MASKED = -1e30
LN2 = 0.6931471805599453
LOG2E = 1.4426950408889634
EPS = 1e-05
SEQ_MAX = 1792
DRIFT = 128
PAD = 128
BLOCK = 256
f32 = jnp.float32
bf16 = jnp.bfloat16


def dot(left, right):
    return jnp.dot(left, right, preferred_element_type=f32)


def dot_nt(left, right):
    return lax.dot_general(left, right, (((1,), (1,)), ((), ())), preferred_element_type=f32)


def dot_tn(left, right):
    return lax.dot_general(left, right, (((0,), (0,)), ((), ())), preferred_element_type=f32)


def split_rows(pair):
    zero = jnp.zeros((HEAD_DIM, pair.shape[1]), pair.dtype)
    return [
        jnp.concatenate([pair[:HEAD_DIM], zero], axis=0),
        jnp.concatenate([zero, pair[HEAD_DIM:]], axis=0),
    ]


def stack_lanes(pair):
    first = lax.broadcasted_iota(jnp.int32, pair.shape, 1) < HEAD_DIM
    zero = jnp.zeros_like(pair)
    return jnp.concatenate([jnp.where(first, pair, zero), jnp.where(first, zero, pair)], axis=0)


def over_range(low, high, body):
    def step(i, carry):
        body(pl.ds(pl.multiple_of(low + i * 128, 128), 128))
        return carry

    lax.fori_loop(0, pl.cdiv(high - low, 128), step, 0)


def over_tiles(info, segments, block, tile):
    def one_segment(segment, carry):
        first, count, low, high = (info[4 * segment + i, block] for i in range(4))

        def full(i, carry):
            tile(pl.multiple_of(first + i * BLOCK, 128), segment, False)
            return carry

        def edge(j, carry):
            i = jnp.where(j < low, j, j - low + high)
            tile(pl.multiple_of(first + i * BLOCK, 128), segment, True)
            return carry

        lax.fori_loop(low, high, full, 0)
        lax.fori_loop(0, low + count - high, edge, 0)
        return carry

    if segments == 1:
        one_segment(0, 0)
    else:
        lax.fori_loop(0, segments, one_segment, 0)


def owned(info, segments, cores, before, length):
    owner = lax.rem(info[4 * segments + 2, 0] + cores - before, cores)
    return pl.ds(pl.multiple_of(owner * length, length), length)


def allowed(row, start, end):
    place = row + lax.broadcasted_iota(jnp.int32, (BLOCK, start.shape[1]), 0)
    return (place >= start) & (place < end)


def pair_cols(head):
    return slice(head // 2 * 128, head // 2 * 128 + 128)


def head_rows(head):
    return slice(head * HEAD_DIM, head * HEAD_DIM + HEAD_DIM)


def attend_kernel(prefix, resume, last, segments, pieces, cores, info, *refs):
    refs = list(refs)
    q, start, end = refs[:3]
    del refs[:3]
    if pieces is None:
        k, v = refs[:2]
        del refs[:2]
    else:
        wk, wv = refs[:2]
        del refs[:2]
        parts = []
        for length, raw in pieces:
            count = cores if raw else 2
            parts.append(refs[:count])
            del refs[:count]
    if prefix:
        pk, pv = refs[:2]
        del refs[:2]
    if resume:
        top_in, total_in, acc_in = refs[:3]
        del refs[:3]
    outs = refs[: 2 if last else 3]
    del refs[: len(outs)]
    if pieces is not None:
        k, v = refs[:2]
        del refs[:2]
    vt = refs.pop(0)
    if last:
        out, lse = outs
        top, total, acc = refs[:3]
        del refs[:3]
    else:
        top, total, acc = outs
    block = pl.program_id(0)
    heads = q.shape[1] // HEAD_DIM
    least, most = info[4 * segments, 0], info[4 * segments + 1, 0]

    def bring(piece, offset, length, sem):
        window = pl.ds(offset, length)
        return (
            pltpu.make_async_copy(piece[0], k.at[window, :], sem.at[0]),
            pltpu.make_async_copy(piece[1], v.at[window, :], sem.at[1]),
        )

    def project(piece, offset, length):
        def rows_at(row, size):
            window = pl.ds(offset + row, size)

            @pl.when((offset + row < most) & (offset + row + size > least))
            def _():
                source = pl.ds(row, size)
                depth = piece[0].shape[1]
                new_k, new_v = 0.0, 0.0
                for core, part in enumerate(piece):
                    some = owned(info, segments, cores, core, depth)
                    value = part[source, :]
                    new_k = new_k + dot(value, wk[some, :])
                    new_v = new_v + dot(value, wv[some, :])
                k[window, :] = new_k.astype(bf16)
                new_v = new_v.astype(bf16)
                v[window, :] = new_v
                vt[:, window] = new_v.T

        def step(i, carry):
            rows_at(pl.multiple_of(i * BLOCK, BLOCK), BLOCK)
            return carry

        full = length // BLOCK
        lax.fori_loop(0, full, step, 0)
        if length % BLOCK:
            rows_at(full * BLOCK, length % BLOCK)

    def turn_over(window):
        vt[:, window] = v[window, :].T

    @pl.when(block == 0)
    def _():
        if pieces is None:
            over_range(least, most, turn_over)
        else:
            offset, ready = 0, []
            for (length, raw), piece in zip(pieces, parts):
                if not raw:
                    ready.append((offset, length))
                    for copy in bring(piece, offset, length, refs[0]):
                        copy.start()
                offset += length
            rest = slice(offset, k.shape[0])
            k[rest, :] = jnp.zeros((k.shape[0] - offset, k.shape[1]), bf16)
            v[rest, :] = jnp.zeros((k.shape[0] - offset, k.shape[1]), bf16)
            vt[:, rest] = jnp.zeros((k.shape[1], k.shape[0] - offset), bf16)
            offset = 0
            for (length, raw), piece in zip(pieces, parts):
                if raw:
                    project(piece, offset, length)
                offset += length
            offset = 0
            for (length, raw), piece in zip(pieces, parts):
                if not raw:
                    for copy in bring(piece, offset, length, refs[0]):
                        copy.wait()
                    over_range(jnp.maximum(least, offset), jnp.minimum(most, offset + length), turn_over)
                offset += length

    qs = []
    for pair in range(heads // 2):
        qs.extend(split_rows(q[:, pair * 128 : pair * 128 + 128].T))
    if resume:
        top[...] = top_in[...]
        total[...] = total_in[...]
        acc[...] = acc_in[...]
    elif prefix:
        there = lax.broadcasted_iota(jnp.int32, (32, BLOCK), 0) < prefix
        for head in range(heads):
            scores = jnp.where(there, dot(pk[:, pair_cols(head)], qs[head]), MASKED)
            peak = jnp.max(scores, axis=0, keepdims=True)
            weights = jnp.exp2(scores - peak)
            top[head : head + 1] = peak
            total[head : head + 1] = jnp.sum(weights, axis=0, keepdims=True)
            turned = pv[:, pair_cols(head)].T
            acc[head_rows(head)] = dot(turned[head_rows(head % 2)], weights.astype(bf16))
    else:
        top[...] = jnp.full(top.shape, MASKED, f32)
        total[...] = jnp.zeros(total.shape, f32)
        acc[...] = jnp.zeros(acc.shape, f32)

    def tile(row, segment, edge):
        window = pl.ds(row, BLOCK)
        if edge:
            seen = pl.ds(segment, 1)
            open_ = allowed(row, start[seen, :], end[seen, :])
        scores = [dot(k[window, pair_cols(head)], qs[head]) for head in range(heads)]
        for head in range(heads):
            score = scores[head]
            if edge:
                score = jnp.where(open_, score, MASKED)
            old = top[head : head + 1]
            peak = jnp.maximum(old, jnp.max(score, axis=0, keepdims=True))
            weights = jnp.exp2(score - peak)
            scale = jnp.exp2(old - peak)
            top[head : head + 1] = peak
            total[head : head + 1] = total[head : head + 1] * scale + jnp.sum(
                weights, axis=0, keepdims=True
            )
            acc[head_rows(head)] = acc[head_rows(head)] * scale + dot(
                vt[head_rows(head), window], weights.astype(bf16)
            )

    over_tiles(info, segments, block, tile)
    if last:
        for pair in range(heads // 2):
            parts = [
                acc[head_rows(head)] * (1.0 / total[head : head + 1])
                for head in (2 * pair, 2 * pair + 1)
            ]
            out[:, pair * 128 : pair * 128 + 128] = (
                jnp.concatenate(parts, axis=0).T.astype(bf16)
            )
        lse[...] = top[...] + jnp.log2(total[...])


def kernel_params():
    return pltpu.CompilerParams(
        dimension_semantics=("arbitrary",), vmem_limit_bytes=60 << 20
    )


class Rows(NamedTuple):
    parts: list
    length: int
    place: int = 0


def attend(query, keys, values, start, end, info, prefix=None, state=None, last=True, weights=None):
    rows, cols = query.shape
    heads = cols // HEAD_DIM
    by_rows = pl.BlockSpec((BLOCK, cols), lambda b, info: (b, 0))
    by_lanes = lambda count: pl.BlockSpec((count, BLOCK), lambda b, info: (0, b))
    whole = lambda count, wide=cols: pl.BlockSpec((count, wide), lambda b, info: (0, 0))
    segments = start.shape[0]
    operands = [query, start, end]
    specs = [by_rows, by_lanes(segments), by_lanes(segments)]
    pieces, cores = None, 1
    if weights is None:
        window = keys.shape[0]
        operands += [keys, values]
        specs += [whole(window)] * 2
    else:
        pieces = tuple(
            (piece.length, True) if isinstance(piece, Rows) else (piece[0].shape[0], False)
            for piece in keys
        )
        window = sum(length for length, raw in pieces) + PAD
        operands += list(weights)
        specs += [whole(weights[0].shape[0])] * 2
        for (length, raw), piece in zip(pieces, keys):
            if raw:
                cores = len(piece.parts)
                operands += list(piece.parts)
                place = piece.place
                specs += [
                    pl.BlockSpec((length, part.shape[1]), lambda b, info, place=place: (place, 0))
                    for part in piece.parts
                ]
            else:
                operands += list(piece)
                specs += [pl.BlockSpec(memory_space=pl.ANY)] * 2
    if prefix is not None:
        operands += [prefix[0], prefix[1]]
        specs += [whole(32), whole(32)]
    state_specs = [by_lanes(heads), by_lanes(heads), by_lanes(cols)]
    if state is not None:
        operands += list(state)
        specs += state_specs
    shape = jax.ShapeDtypeStruct
    scratch = [pltpu.VMEM((cols, window), bf16)]
    if last:
        outs = [shape((rows, cols), bf16), shape((heads, rows), f32)]
        out_specs = [by_rows, by_lanes(heads)]
        scratch += [pltpu.VMEM((n, BLOCK), f32) for n in (heads, heads, cols)]
    else:
        outs = [shape((n, rows), f32) for n in (heads, heads, cols)]
        out_specs = list(state_specs)
    if weights is not None:
        outs += [shape((window, cols), bf16)] * 2
        out_specs += [whole(window)] * 2
        scratch.append(pltpu.SemaphoreType.DMA((2,)))
    return pl.pallas_call(
        functools.partial(
            attend_kernel, 0 if prefix is None else prefix[2], state is not None, last, segments,
            pieces, cores,
        ),
        out_shape=tuple(outs),
        grid_spec=pltpu.PrefetchScalarGridSpec(
            num_scalar_prefetch=1,
            grid=(rows // BLOCK,),
            in_specs=specs,
            out_specs=tuple(out_specs),
            scratch_shapes=scratch,
        ),
        compiler_params=kernel_params(),
    )(info, *operands)


def attend_back_kernel(prefix, resume, own, final, cuts, cores, segments, info, *refs):
    refs = list(refs)
    q, d_out, out, k, v, start, end, lse, wk, wv = refs[:10]
    del refs[:10]
    if prefix:
        pk, pv = refs[:2]
        del refs[:2]
    if resume:
        dq_in = refs.pop(0)
    if own:
        wq = refs.pop(0)
    pieces = len(cuts) - 1
    grads = [refs[i * cores : i * cores + cores] for i in range(pieces)]
    del refs[: pieces * cores]
    if prefix:
        dpk, dpv = refs[:2]
        del refs[:2]
    if not own:
        dq_out = refs.pop(0)
    kt, dk, dv = refs[:3]
    del refs[:3]
    if own:
        dq, dq_low = refs
    elif final:
        (dq,) = refs
    else:
        dq = dq_out
    block = pl.program_id(0)
    heads = q.shape[1] // HEAD_DIM
    pairs = heads // 2

    @pl.when(block == 0)
    def _():
        def prepare(window):
            kt[:, window] = k[window, :].T
            dk[window, :] = jnp.zeros((128, dk.shape[1]), f32)
            dv[window, :] = jnp.zeros((128, dv.shape[1]), f32)

        over_range(info[4 * segments, 0], info[4 * segments + 1, 0], prepare)
        if prefix:
            dpk[...] = jnp.zeros(dpk.shape, f32)
            dpv[...] = jnp.zeros(dpv.shape, f32)

    qs, ds, delta, q_stack, d_stack = [], [], [], [], []
    for pair in range(pairs):
        cols = slice(pair * 128, pair * 128 + 128)
        q_pair, d_pair = q[:, cols], d_out[:, cols]
        qs.extend(split_rows(q_pair.T))
        ds.extend(split_rows(d_pair.T))
        both = (d_pair.astype(f32) * out[:, cols].astype(f32)).T
        delta.append(jnp.sum(both[:HEAD_DIM], axis=0, keepdims=True))
        delta.append(jnp.sum(both[HEAD_DIM:], axis=0, keepdims=True))
        q_stack.append(stack_lanes(q_pair))
        d_stack.append(stack_lanes(d_pair))
    if resume:
        dq[...] = dq_in[...]
    else:
        dq[...] = jnp.zeros(dq.shape, f32)
    if prefix:
        there = lax.broadcasted_iota(jnp.int32, (32, BLOCK), 0) < prefix
        for pair in range(pairs):
            cols = slice(pair * 128, pair * 128 + 128)
            turned = pk[:, cols].T
            ws, gs = [], []
            for head in (2 * pair, 2 * pair + 1):
                scores = dot(pk[:, cols], qs[head])
                weights = jnp.where(there, jnp.exp2(scores - lse[head : head + 1]), 0.0)
                grad = (weights * (dot(pv[:, cols], ds[head]) - delta[head])).astype(bf16)
                dq[head_rows(head)] += dot(turned[head_rows(head % 2)], grad)
                ws.append(weights.astype(bf16))
                gs.append(grad)
            dpv[:, cols] += dot(jnp.concatenate(ws, axis=1), d_stack[pair])
            dpk[:, cols] += dot(jnp.concatenate(gs, axis=1), q_stack[pair]) * LN2

    def tile(row, segment, edge):
        window = pl.ds(row, BLOCK)
        if edge:
            seen = pl.ds(segment, 1)
            open_ = allowed(row, start[seen, :], end[seen, :])
        scores = [dot(k[window, pair_cols(head)], qs[head]) for head in range(heads)]
        inner = [dot(v[window, pair_cols(head)], ds[head]) for head in range(heads)]
        for pair in range(pairs):
            cols = slice(pair * 128, pair * 128 + 128)
            ws, gs = [], []
            for head in (2 * pair, 2 * pair + 1):
                weights = jnp.exp2(scores[head] - lse[head : head + 1])
                if edge:
                    weights = jnp.where(open_, weights, 0.0)
                grad = (weights * (inner[head] - delta[head])).astype(bf16)
                dq[head_rows(head)] += dot(kt[head_rows(head), window], grad)
                ws.append(weights.astype(bf16))
                gs.append(grad)
            dv[window, cols] += dot(jnp.concatenate(ws, axis=1), d_stack[pair])
            dk[window, cols] += dot(jnp.concatenate(gs, axis=1), q_stack[pair])

    over_tiles(info, segments, block, tile)
    if own:
        dq_low[pl.ds(pl.multiple_of(block * BLOCK, BLOCK), BLOCK), :] = (
            (dq[...] * 0.125).T.astype(bf16)
        )
    elif final:
        dq_out[...] = (dq[...] * 0.125).T.astype(bf16)

    @pl.when(block == pl.num_programs(0) - 1)
    def _():
        least, most = info[4 * segments, 0], info[4 * segments + 1, 0]

        def project(row, size, piece, offset):
            window = pl.ds(row, size)
            target = pl.ds(offset, size)
            touched = (row < most) & (row + size > least)
            width = grads[piece][0].shape[1]

            @pl.when(touched)
            def _():
                place = row + lax.broadcasted_iota(jnp.int32, (size, dk.shape[1]), 0)
                there = (place >= least) & (place < most)
                dk_low = jnp.where(there, dk[window, :] * LN2, 0.0).astype(bf16)
                dv_low = jnp.where(there, dv[window, :], 0.0).astype(bf16)
                for core in range(cores):
                    part = owned(info, segments, cores, core, width)
                    value = dot_nt(dk_low, wk[part, :]) + dot_nt(dv_low, wv[part, :])
                    if own:
                        value += dot_nt(dq_low[target, :], wq[part, :])
                    grads[piece][core][target, :] = value.astype(bf16)

            @pl.when(jnp.logical_not(touched))
            def _():
                for core in range(cores):
                    value = jnp.zeros((size, width), f32)
                    if own:
                        part = owned(info, segments, cores, core, width)
                        value = dot_nt(dq_low[target, :], wq[part, :])
                    grads[piece][core][target, :] = value.astype(bf16)

        for piece in range(pieces):
            length = cuts[piece + 1] - cuts[piece]
            whole = length // BLOCK

            def step(i, carry, piece=piece):
                offset = pl.multiple_of(i * BLOCK, BLOCK)
                project(pl.multiple_of(cuts[piece] + offset, 128), BLOCK, piece, offset)
                return carry

            lax.fori_loop(0, whole, step, 0)
            rest = length - whole * BLOCK
            if rest:
                project(cuts[piece] + whole * BLOCK, rest, piece, whole * BLOCK)


def attend_back(
    query, d_out, out, keys, values, start, end, lse, info, key_weight, value_weight, cuts, cores,
    prefix=None, state=None, query_weight=None, final=False,
):
    rows, cols = query.shape
    window = cuts[-1] + (0 if query_weight is not None else PAD)
    width = key_weight.shape[0]
    heads = cols // HEAD_DIM
    own = query_weight is not None
    segments = start.shape[0]
    by_rows = pl.BlockSpec((BLOCK, cols), lambda b, info: (b, 0))
    by_lanes = lambda count: pl.BlockSpec((count, BLOCK), lambda b, info: (0, b))
    whole = lambda count, wide=cols: pl.BlockSpec((count, wide), lambda b, info: (0, 0))
    operands = [query, d_out, out, keys, values, start, end, lse, key_weight, value_weight]
    specs = [by_rows] * 3 + [whole(window)] * 2 + [by_lanes(segments)] * 2 + [by_lanes(heads)]
    specs += [whole(width)] * 2
    if prefix is not None:
        operands += [prefix[0], prefix[1]]
        specs += [whole(32), whole(32)]
    if state is not None:
        operands.append(state)
        specs.append(by_lanes(cols))
    if own:
        operands.append(query_weight)
        specs.append(whole(width))
    shape = jax.ShapeDtypeStruct
    outs, out_specs = [], []
    for piece in range(len(cuts) - 1):
        length = cuts[piece + 1] - cuts[piece]
        outs += [shape((length, width // cores), bf16)] * cores
        out_specs += [whole(length, width // cores)] * cores
    if prefix is not None:
        outs += [shape((32, cols), f32)] * 2
        out_specs += [whole(32)] * 2
    scratch = [
        pltpu.VMEM((cols, window), bf16),
        pltpu.VMEM((window, cols), f32),
        pltpu.VMEM((window, cols), f32),
    ]
    if own:
        scratch += [pltpu.VMEM((cols, BLOCK), f32), pltpu.VMEM((rows, cols), bf16)]
    elif final:
        scratch.append(pltpu.VMEM((cols, BLOCK), f32))
        outs.append(shape((rows, cols), bf16))
        out_specs.append(by_rows)
    else:
        outs.append(shape((cols, rows), f32))
        out_specs.append(by_lanes(cols))
    result = pl.pallas_call(
        functools.partial(
            attend_back_kernel,
            0 if prefix is None else prefix[2], state is not None, own, final, tuple(cuts), cores,
            segments,
        ),
        out_shape=tuple(outs),
        grid_spec=pltpu.PrefetchScalarGridSpec(
            num_scalar_prefetch=1,
            grid=(rows // BLOCK,),
            in_specs=specs,
            out_specs=tuple(out_specs),
            scratch_shapes=scratch,
        ),
        compiler_params=kernel_params(),
    )(info, *operands)
    pieces = [
        list(result[i * cores : i * cores + cores]) for i in range(len(cuts) - 1)
    ]
    return pieces, *result[(len(cuts) - 1) * cores :]


class Span(NamedTuple):
    segments: tuple
    step: int = 128
    causal: bool = True


def spans_kernel(spans, total, rows, tgt, mem, at, *refs):
    here, core = at[0], at[1]
    place = here + lax.broadcasted_iota(jnp.int32, (1, rows), 1)

    def one(j, carry):
        begin, mem_begin, start, mem_start, mem_end = carry
        end, mem_stop = begin + tgt[j], mem_begin + mem[j]
        past = place >= end
        start = jnp.where(past, end, start)
        mem_start = jnp.where(past, mem_stop, mem_start)
        mem_end = jnp.where(place >= begin, mem_stop, mem_end)
        return end, mem_stop, start, mem_start, mem_end

    zero = jnp.zeros((1, rows), jnp.int32)
    begin, _, start, mem_start, mem_end = lax.fori_loop(
        0, tgt.shape[0], one, (0, 0, zero, zero, zero)
    )
    mem_end = jnp.where(place >= begin, total, mem_end)
    blocks = rows // BLOCK

    def least(value, block):
        part = value[:, block * BLOCK : block * BLOCK + BLOCK].astype(f32)
        return jnp.min(part).astype(jnp.int32)

    def most(value, block):
        part = value[:, block * BLOCK : block * BLOCK + BLOCK].astype(f32)
        return jnp.max(part).astype(jnp.int32)

    ends = [
        [(least(value, b), most(value, b)) for b in range(blocks)]
        for value in (start - here, mem_start - here, mem_end - here)
    ]
    for i, span in enumerate(spans):
        starts_out, ends_out, info = refs[3 * i : 3 * i + 3]
        lowest, highest = 1 << 20, 0
        for segment, (base, low, high) in enumerate(span.segments):
            clip = lambda value: jnp.clip(value + base, low, high)
            if span.causal:
                lows, highs = start - here, place - here + 1
                corners = [(ends[0][b], (b * BLOCK + 1, b * BLOCK + BLOCK)) for b in range(blocks)]
            else:
                lows, highs = mem_start - here, mem_end - here
                corners = [(ends[1][b], ends[2][b]) for b in range(blocks)]
            starts_out[segment : segment + 1, :] = clip(lows)
            ends_out[segment : segment + 1, :] = clip(highs)
            for b, ((s0, s1), (e0, e1)) in enumerate(corners):
                s0, s1, e0, e1 = clip(s0), clip(s1), clip(e0), clip(e1)
                some = e1 > s0
                first = jnp.where(some, s0 // span.step * span.step, 0)
                count = jnp.where(some, (e1 - first + BLOCK - 1) // BLOCK, 0)
                from_ = jnp.clip((s1 - first + BLOCK - 1) // BLOCK, 0, count)
                to = jnp.clip((e0 - first) // BLOCK, from_, count)
                for row, value in enumerate((first, count, from_, to)):
                    info[4 * segment + row, b] = value
                lowest = jnp.where(some, jnp.minimum(lowest, first), lowest)
                highest = jnp.where(some, jnp.maximum(highest, first + count * BLOCK), highest)
        tail = 4 * len(span.segments)
        for b in range(blocks):
            info[tail, b] = jnp.minimum(lowest, highest)
            info[tail + 1, b] = highest
            info[tail + 2, b] = core
            info[tail + 3, b] = 0


def see(spans, total, rows, tgt, mem, at):
    outs, specs = [], []
    for span in spans:
        count = len(span.segments)
        outs += [jax.ShapeDtypeStruct((count, rows), jnp.int32)] * 2
        outs.append(jax.ShapeDtypeStruct((4 * count + 4, rows // BLOCK), jnp.int32))
        specs += [pl.BlockSpec((count, rows), lambda i, *scalars: (0, 0))] * 2
        specs.append(pl.BlockSpec(memory_space=pltpu.SMEM))
    result = pl.pallas_call(
        functools.partial(spans_kernel, spans, total, rows),
        out_shape=tuple(outs),
        grid_spec=pltpu.PrefetchScalarGridSpec(
            num_scalar_prefetch=3, grid=(1,), in_specs=[], out_specs=tuple(specs)
        ),
    )(tgt, mem, at)
    return [result[3 * i : 3 * i + 3] for i in range(len(spans))]


def norm_parts(value):
    center = value - jnp.mean(value, axis=-1, keepdims=True)
    scale = lax.rsqrt(jnp.mean(center * center, axis=-1, keepdims=True) + EPS)
    return center * scale, scale


def norm_back(normal, scale, grad):
    return scale * (
        grad
        - jnp.mean(grad, axis=-1, keepdims=True)
        - normal * jnp.mean(grad * normal, axis=-1, keepdims=True)
    )


def gelu_pair(value):
    size = jnp.abs(value)
    bell = jnp.exp(-0.5 * value * value)
    under = 1.0 + (0.3275911 * 0.7071067811865476) * size
    t = pl.reciprocal(under, approx=True)
    t = t * (2.0 - under * t)
    poly = ((((1.061405429 * t - 1.453152027) * t + 1.421413741) * t - 0.284496736) * t + 0.254829592) * t
    tail = 0.5 * poly * bell
    cdf = jnp.where(value >= 0, 1.0 - tail, tail)
    return value * cdf, cdf + value * (0.3989422804014327 * bell)


def ffn_kernel(cores, chunk, core, *refs):
    refs = list(refs)

    def take(count):
        taken = refs[:count]
        del refs[:count]
        return taken

    crossed = take(cores)
    cross_outs = take(cores)
    first, cot = take(2)
    downs = take(cores)
    biases = take(cores)
    ups = take(cores)
    (up_bias,) = take(1)
    hins, houts = take(2)
    cross_outs, downs, ups = ([ref.at[0] for ref in part] for part in (cross_outs, downs, ups))
    out, d_cross = take(2)
    d_crossed = take(cores)
    adapter_grads = take(cores)
    hin, hout, in_sem, out_sem, slope, bufs0, bufs1, branch, second, second_low, adapted, down_slope, low = refs
    per = hins.shape[2] // chunk
    count = per * cores
    adapt = downs[0].shape[1]

    def copies(j):
        c, i = divmod(j, per)
        part = pl.ds(i * chunk, chunk)
        return (
            pltpu.make_async_copy(hins.at[c, :, part], hin.at[j], in_sem.at[j]),
            pltpu.make_async_copy(houts.at[c, part, :], hout.at[j], out_sem.at[j]),
        )

    for j in range(count):
        for copy in copies(j):
            copy.start()
    total = first[...]
    for value, weight in zip(crossed, cross_outs):
        total = total + dot(value[...], weight[...])
    normal, scale2 = norm_parts(total)
    second[...] = normal
    second_low[...] = normal.astype(bf16)

    wide = 4.0 * up_bias[...]
    acc = jnp.zeros(branch.shape, f32)
    for c in range(cores):
        part = slice(c * adapt, (c + 1) * adapt)
        value, grad = gelu_pair(dot(second_low[...], downs[c][...]) + biases[c][...])
        adapted[:, part] = value.astype(bf16)
        down_slope[:, part] = grad
        acc = acc + dot(adapted[:, part], ups[c][...])
    branch[...] = 4.0 * acc + wide

    for j in range(count):
        for copy in copies(j):
            copy.wait()
    bufs0[...] = dot(second_low[...], hin[0])

    def forward(j, now, later):
        later[...] = dot(second_low[...], hin[jnp.minimum(j + 1, count - 1)])
        value, grad = gelu_pair(now[...])
        slope[j] = grad.astype(bf16)
        branch[...] += dot(value.astype(bf16), hout[j])

    def forward_two(i, _):
        forward(2 * i, bufs0, bufs1)
        forward(2 * i + 1, bufs1, bufs0)
        return 0

    lax.fori_loop(0, count // 2, forward_two, 0)
    normal, scale = norm_parts(second[...] + branch[...])
    out[...] = normal.astype(bf16)
    d_third = norm_back(normal, scale, cot[...].astype(f32))
    branch[...] = d_third
    low[...] = d_third.astype(bf16)
    up_sum = 4.0 * jnp.sum(low[...].astype(f32), axis=0, keepdims=True)
    line = lax.broadcasted_iota(jnp.int32, (16, up_sum.shape[1]), 0)

    def backward(j):
        value = (slope[j].astype(f32) * dot_nt(low[...], hout[j])).astype(bf16)
        branch[...] += dot_nt(value, hin[j])

    def backward_two(i, _):
        backward(2 * i)
        backward(2 * i + 1)
        return 0

    lax.fori_loop(0, count // 2, backward_two, 0)
    total = branch[...]
    for c in range(cores):
        part = slice(c * adapt, (c + 1) * adapt)
        value = (down_slope[:, part] * (4.0 * dot_nt(low[...], ups[c][...]))).astype(bf16)
        total = total + dot_nt(value, downs[c][...])
        adapter_grads[c][adapt : 2 * adapt, :] = dot_tn(value, second_low[...]).astype(bf16)
        adapter_grads[c][:adapt, :] = (4.0 * dot_tn(adapted[:, part], low[...])).astype(bf16)
        down_sum = jnp.sum(value.astype(f32), axis=0, keepdims=True)
        down_sum = jnp.concatenate(
            [down_sum, jnp.zeros((1, up_sum.shape[1] - adapt), f32)], axis=1
        )
        biases_low = jnp.where(line == 0, up_sum, jnp.where(line == 1, down_sum, 0.0))
        adapter_grads[c][2 * adapt :, :] = biases_low.astype(bf16)
    d_second = norm_back(second[...], scale2, total)
    d_cross[...] = d_second
    for result, weight in zip(d_crossed, cross_outs):
        result[...] = dot_nt(d_second.astype(bf16), weight[...]).astype(bf16)


def at_core(cores, rows, width):
    return pl.BlockSpec((rows, width), lambda i, core: (core[0], 0))


def down_from_core(cores, shape):
    def spec(k):
        return pl.BlockSpec(
            (1,) + shape, lambda i, core: (lax.rem(core[0] + cores - k, cores), 0, 0)
        )

    return [spec(k) for k in range(cores)]


def one_step(kernel, core, operands, specs, outs, scratch):
    whole = lambda shape: pl.BlockSpec(shape, lambda i, core: (0,) * len(shape))
    specs = [whole(op.shape) if spec is None else spec for op, spec in zip(operands, specs)]
    return pl.pallas_call(
        kernel,
        out_shape=tuple(outs),
        grid_spec=pltpu.PrefetchScalarGridSpec(
            num_scalar_prefetch=1,
            grid=(1,),
            in_specs=specs,
            out_specs=tuple(whole(out.shape) for out in outs),
            scratch_shapes=scratch,
        ),
        compiler_params=kernel_params(),
    )(core, *operands)


def feed_forward(core, crossed, crossed_others, cross_outs, first, cot, downs, biases, ups, up_bias, hins, houts):
    rows, width = first.shape
    cores, _, hidden = hins.shape
    adapt = downs.shape[2]
    heads = crossed.shape[1]
    chunk = min(512, hidden)
    count = cores * hidden // chunk
    hbm = pl.BlockSpec(memory_space=pl.ANY)
    operands = [crossed] + list(crossed_others)
    specs = [at_core(cores, rows, heads)] + [None] * (cores - 1)
    operands += [cross_outs] * cores + [first, cot]
    specs += down_from_core(cores, cross_outs.shape[1:]) + [None, at_core(cores, rows, width)]
    operands += [downs] * cores + [bias[None] for bias in biases] + [ups] * cores + [up_bias[None]]
    specs += down_from_core(cores, downs.shape[1:]) + [None] * cores
    specs += down_from_core(cores, ups.shape[1:]) + [None]
    operands += [hins, houts]
    specs += [hbm, hbm]
    shape = jax.ShapeDtypeStruct
    outs = (
        [shape((rows, width), bf16), shape((rows, width), f32)]
        + [shape((rows, heads), bf16)] * cores
        + [shape((2 * adapt + 16, width), bf16)] * cores
    )
    scratch = [
        pltpu.VMEM((count, width, chunk), bf16),
        pltpu.VMEM((count, chunk, width), bf16),
        pltpu.SemaphoreType.DMA((count,)),
        pltpu.SemaphoreType.DMA((count,)),
        pltpu.VMEM((count, rows, chunk), bf16),
        pltpu.VMEM((rows, chunk), f32),
        pltpu.VMEM((rows, chunk), f32),
        pltpu.VMEM((rows, width), f32),
        pltpu.VMEM((rows, width), f32),
        pltpu.VMEM((rows, width), bf16),
        pltpu.VMEM((rows, adapt * cores), bf16),
        pltpu.VMEM((rows, adapt * cores), f32),
        pltpu.VMEM((rows, width), bf16),
    ]
    result = one_step(
        functools.partial(ffn_kernel, cores, chunk), core, operands, specs, outs, scratch
    )
    at = 2 + cores
    return result[0], result[1], list(result[2:at]), list(result[at:])


def after_self_kernel(cores, core, *refs):
    refs = list(refs)
    attended, refs = refs[:cores], refs[cores:]
    outputs, refs = refs[:cores], refs[cores:]
    queries, refs = refs[:cores], refs[cores:]
    tokens, first, scale = refs[:3]
    total = tokens[...].astype(f32)
    for value, weight in zip(attended, outputs):
        total = total + dot(value[...], weight[0])
    normal, inverse = norm_parts(total)
    first[...] = normal
    scale[...] = inverse
    low = normal.astype(bf16)
    for result, weight in zip(refs[3:], queries):
        result[...] = (dot(low, weight[0]) * (0.125 * LOG2E)).astype(bf16)


def after_self(core, attended, attended_others, outputs, queries, tokens):
    cores, heads, width = outputs.shape
    rows = tokens.shape[0] // cores
    operands = [attended] + list(attended_others) + [outputs] * cores + [queries] * cores + [tokens]
    specs = [at_core(cores, rows, heads)] + [None] * (cores - 1)
    specs += down_from_core(cores, outputs.shape[1:]) + down_from_core(cores, queries.shape[1:])
    specs += [at_core(cores, rows, width)]
    shape = jax.ShapeDtypeStruct
    outs = [shape((rows, width), f32), shape((rows, 1), f32)] + [shape((rows, heads), bf16)] * cores
    result = one_step(
        functools.partial(after_self_kernel, cores), core, operands, specs, outs, []
    )
    return result[0], result[1], list(result[2:])


def before_self_kernel(cores, core, *refs):
    refs = list(refs)
    grads, refs = refs[:cores], refs[cores:]
    queries, refs = refs[:cores], refs[cores:]
    outputs, refs = refs[:cores], refs[cores:]
    d_cross, first, scale, kept = refs[:4]
    sent, refs = refs[4 : 3 + cores], refs[3 + cores :]
    d_attended, d_tokens = refs[:cores], refs[cores]
    total = d_cross[...]
    for value, weight in zip(grads, queries):
        total = total + dot_nt(value[...], weight[0])
    total = norm_back(first[...], scale[...], total)
    d_tokens[...] = total
    low = total.astype(bf16)
    for result, weight in zip(d_attended, outputs):
        result[...] = dot_nt(low, weight[0]).astype(bf16)
    width = kept.shape[1]
    for k, result in enumerate([kept] + sent):
        owner = lax.rem(core[0] + cores - k, cores)
        part = pl.ds(pl.multiple_of(owner * width, width), width)
        result[...] = d_tokens[:, part].astype(result.dtype)


def before_self(core, grads, grads_others, queries, outputs, d_cross, first, scale):
    cores, heads, width = outputs.shape
    rows = first.shape[0]
    operands = [grads] + list(grads_others) + [queries] * cores + [outputs] * cores
    operands += [d_cross, first, scale]
    specs = [at_core(cores, rows, heads)] + [None] * (cores - 1)
    specs += down_from_core(cores, queries.shape[1:]) + down_from_core(cores, outputs.shape[1:])
    specs += [None] * 3
    shape = jax.ShapeDtypeStruct
    outs = [shape((rows, width // cores), f32)] + [shape((rows, width // cores), bf16)] * (cores - 1)
    outs += [shape((rows, heads), bf16)] * cores
    result = one_step(
        functools.partial(before_self_kernel, cores), core, operands, specs, outs,
        [pltpu.VMEM((rows, width), f32)],
    )
    return list(result[:cores]), list(result[cores:])


def beside_kernel(core, *refs):
    which = pl.program_id(0)
    for k, part in enumerate(refs[:-1]):

        @pl.when(which == k)
        def _(part=part):
            refs[-1][...] = part[...].astype(f32)


def beside(core, parts):
    rows, width = parts[0].shape
    cores = len(parts)
    count = 2

    def part_spec(k):
        def place(which, block, core):
            return (jnp.where(which == k, block, jnp.where(which < k, 0, count - 1)), 0)

        return pl.BlockSpec((rows // count, width), place)

    return pl.pallas_call(
        beside_kernel,
        out_shape=jax.ShapeDtypeStruct((rows, cores * width), f32),
        grid_spec=pltpu.PrefetchScalarGridSpec(
            num_scalar_prefetch=1,
            grid=(cores, count),
            in_specs=[part_spec(k) for k in range(cores)],
            out_specs=pl.BlockSpec(
                (rows // count, width),
                lambda which, block, core: (block, lax.rem(core[0] + cores - which, cores)),
            ),
        ),
    )(core, *parts)


def add_kernel(count, each, cut, *refs):
    for i in range(count):
        total = refs[i * each][...].astype(f32)
        for ref in refs[i * each + 1 : i * each + each]:
            total = total + ref[...].astype(f32)
        if cut is None:
            refs[count * each + i][...] = total.astype(bf16)
        else:
            refs[each][...] = total[:cut].astype(bf16)
            refs[each + 1][...] = total[cut:]


def add_up(lists, cut=None):
    each = len(lists[0])
    shape = jax.ShapeDtypeStruct
    outs = [shape(parts[0].shape, bf16) for parts in lists]
    if cut is not None:
        rows, width = lists[0][0].shape
        outs = [shape((cut, width), bf16), shape((rows - cut, width), f32)]
    return pl.pallas_call(
        functools.partial(add_kernel, len(lists), each, cut),
        out_shape=tuple(outs),
        compiler_params=pltpu.CompilerParams(vmem_limit_bytes=60 << 20),
    )(*[part for parts in lists for part in parts])


SMALL = 48


def pack_kernel(count, *refs):
    parts, refs = refs[:count], refs[count:]
    keys, values, biases, out = refs
    rows = parts[0].shape[0]
    total = parts[0][...].astype(f32)
    for part in parts[1:]:
        total = total + part[...].astype(f32)
    out[:rows, :] = total.astype(bf16)
    out[rows : rows + 32, :] = jnp.zeros((32, out.shape[1]), bf16)
    cols = keys.shape[1]
    out[rows : rows + 32, :cols] = keys[...].astype(bf16)
    out[rows : rows + 32, cols : 2 * cols] = values[...].astype(bf16)
    out[rows + 32 :, :] = biases[...].astype(bf16)


def pack(parts, keys, values, biases):
    rows, width = parts[0].shape
    return pl.pallas_call(
        functools.partial(pack_kernel, len(parts)),
        out_shape=jax.ShapeDtypeStruct((rows + SMALL, width), bf16),
    )(*parts, keys, values, biases)


def gather_kernel(count, rows, last, place, *refs):
    parts, refs = refs[:count], refs[count:]
    total = parts[0][rows:, :].astype(f32)
    for part in parts[1:]:
        total = total + part[rows:, :].astype(f32)
    if last is None:
        (out,) = refs
        joined = out
        out[count * rows :, :] = total.astype(bf16)
    else:
        keys, values, down, down_bias, up, up_bias, joined = refs
        prefix, cols = keys.shape
        keys[...] = total[:prefix, :cols]
        values[...] = total[:prefix, cols : 2 * cols]
        up_bias[...] = total[32:33]
        down_bias[...] = total[33:34, : down_bias.shape[1]]
    for k, part in enumerate(parts):
        owner = jnp.bitwise_xor(place[0], k)
        joined[pl.ds(pl.multiple_of(owner * rows, 16), rows), :] = part[:rows, :]
    if last is not None:
        up[...] = joined[: up.shape[0], :].astype(f32)
        down[...] = joined[up.shape[0] :, :].astype(f32).T


def gather_rows(place, parts, last):
    count = len(parts)
    length, width = parts[0].shape
    rows = length - SMALL
    shape = jax.ShapeDtypeStruct
    if last is None:
        outs, scratch = [shape((count * rows + SMALL, width), bf16)], []
    else:
        prefix, cols, adapt = last
        outs = [
            shape((prefix, cols), f32),
            shape((prefix, cols), f32),
            shape((width, adapt), f32),
            shape((1, adapt), f32),
            shape((adapt, width), f32),
            shape((1, width), f32),
        ]
        scratch = [pltpu.VMEM((count * rows, width), bf16)]
    return one_step(
        functools.partial(gather_kernel, count, rows, last),
        place,
        parts,
        [None] * count,
        outs,
        scratch,
    )


def product(left, right):
    return jnp.dot(left, right, preferred_element_type=f32)


def turn(value, distance):
    size = lax.axis_size("head")
    return lax.ppermute(value, "head", [(i, (i + distance) % size) for i in range(size)])


def others(value):
    return [turn(value, k) for k in range(1, lax.axis_size("head"))]


def in_order(parts, axis):
    size = len(parts)
    core = lax.axis_index("head")
    if size == 2:
        first, second = parts
        return jnp.where(
            core == 0,
            jnp.concatenate([first, second], axis=axis),
            jnp.concatenate([second, first], axis=axis),
        )
    ring = jnp.concatenate([parts[-k % size] for k in range(size)] * 2, axis=axis)
    length = parts[0].shape[axis]
    return lax.dynamic_slice_in_dim(ring, (size - core) % size * length, size * length, axis)


def shift(value, distance):
    devices = range(lax.axis_size("seq"))
    return lax.ppermute(value, "seq", [(i, i + distance) for i in devices if i + distance in devices])


def after(value, *first):
    return lax.optimization_barrier((value, first))[0]


class Ring:
    def __init__(self, size, step):
        self.size, self.step = size, step
        self.place = lax.axis_index("seq") // step % size

    def exchange(self, values):
        pairs = [[(i, i ^ k * self.step) for i in range(lax.axis_size("seq"))] for k in range(self.size)]
        return [lax.ppermute(values[k], "seq", pairs[k]) for k in range(1, self.size)]

    def cut(self, value, k):
        length = value.shape[0] // self.size
        return lax.dynamic_slice_in_dim(value, (self.place ^ k) * length, length, 0)

    def scatter(self, value):
        return self.exchange([self.cut(value, k) for k in range(self.size)])


def on_device(
    tokens,
    memory,
    cotangent,
    tgt_lengths,
    mem_lengths,
    self_query,
    self_key,
    self_value,
    self_output,
    cross_query,
    cross_key,
    cross_value,
    cross_output,
    hidden_in,
    hidden_out,
    prefix_keys,
    prefix_values,
    adapter_down,
    adapter_down_bias,
    adapter_up,
    adapter_up_bias,
):
    rows, width = tokens.shape
    cols = self_query.shape[1]
    prefix = prefix_keys.shape[0]
    shards = lax.axis_size("seq")
    position = lax.axis_index("seq")
    core = lax.axis_index("head")
    cores = lax.axis_size("head")
    total = rows * shards
    core_index = jnp.reshape(core, (1,)).astype(jnp.int32)

    def part_of(value, owner, axis=0):
        length = value.shape[axis] // cores
        return lax.dynamic_slice_in_dim(value, owner % cores * length, length, axis)

    def mine(value, axis=0):
        return part_of(value, core, axis)

    def dealt(parts):
        return [parts[0]] + [turn(parts[k], -k) for k in range(1, cores)]

    def over_cores(parts):
        arrived = [part.astype(f32) for part in dealt(parts)]
        return sum(arrived[1:], arrived[0])

    self_far = min(max(-(-(SEQ_MAX - rows) // 128) * 128, 0), rows)
    cross_far = min(max(-(-(SEQ_MAX + DRIFT - rows) // 128) * 128, 0), rows)
    self_base = rows + self_far
    far_rows = 2 * cross_far
    at = jnp.stack([position * rows, core]).astype(jnp.int32)
    self_seen, own_seen, halo_seen, main_seen, far_seen = see(
        (
            Span(((self_base, 0, self_base + rows),)),
            Span(((0, 0, rows),), BLOCK),
            Span(((self_base, 0, self_base),)),
            Span(((rows, 0, 3 * rows),), causal=False),
            Span(
                ((rows + cross_far, 0, cross_far), (cross_far - 2 * rows, cross_far, far_rows)),
                causal=False,
            ),
        ),
        total,
        rows,
        tgt_lengths,
        mem_lengths,
        at,
    )

    tokens_cols = mine(tokens, 1)
    tokens_end = tokens_cols[rows - self_far :]
    token_near = shift(tokens_cols, 1)
    token_far = shift(tokens_end, 2)
    down_biases = [adapter_down_bias] + others(adapter_down_bias)

    prefix_pad = ((0, 32 - prefix), (0, 0))
    prefix_rows = (
        jnp.pad(prefix_keys.astype(bf16), prefix_pad),
        jnp.pad(prefix_values.astype(bf16), prefix_pad),
        prefix,
    )

    query = (product(tokens, self_query) * (0.125 * LOG2E)).astype(bf16)

    own_keys = product(tokens, self_key).astype(bf16)
    own_values = product(tokens, self_value).astype(bf16)

    def all_cores(value, *first):
        return lax.all_gather(after(value, *first), "head", axis=0)

    self_outputs = all_cores(self_output, query)
    cross_queries = all_cores(cross_query, query)
    arrived = (token_near, token_far)
    ready = (query, own_keys, own_values, self_seen)
    arrived, ready = lax.optimization_barrier((arrived, ready))
    token_near, token_far = arrived
    query, own_keys, own_values, self_seen = ready
    memory_late = after(memory, token_near)
    memory_cols = mine(memory_late, 1)
    memory_keys = product(memory_late, cross_key).astype(bf16)
    memory_values = product(memory_late, cross_value).astype(bf16)

    token_near = [token_near] + others(token_near)
    token_far = [token_far] + others(token_far)
    memory_near = (
        shift(after(memory_cols, token_near, token_far), 1),
        shift(after(memory_cols, token_near, token_far), -1),
    )
    attended, self_lse, self_keys, self_values = attend(
        after(query, memory_keys, memory_values),
        [Rows(token_far, self_far), Rows(token_near, rows), (own_keys, own_values)],
        None,
        *self_seen,
        prefix_rows,
        None,
        True,
        (self_key, self_value),
    )

    def to_rows(value):
        return [turn(part_of(value, core + k), k) for k in range(1, cores)]

    def to_heads(parts):
        parts = [parts[0]] + [turn(parts[k], -k) for k in range(1, cores)]
        return in_order([parts[-k % cores] for k in range(cores)], 0)

    cross_outputs = all_cores(cross_output, memory_keys)
    hidden_ins = all_cores(hidden_in, memory_keys)
    hidden_outs = all_cores(hidden_out, memory_keys)
    downs = all_cores(after(adapter_down, memory_keys).astype(bf16))
    ups = all_cores(after(adapter_up, memory_keys).astype(bf16))
    attended_rows = to_rows(attended)
    attended_rows, memory_near = lax.optimization_barrier((attended_rows, memory_near))
    memory_near = [[part] + others(part) for part in memory_near]
    memory_far = (
        shift(after(memory_cols[rows - cross_far :], memory_near), 2),
        shift(after(memory_cols[:cross_far], memory_near), -2),
    )
    first, first_scale, cross_q = after_self(
        core_index, attended, attended_rows, self_outputs, cross_queries, tokens
    )

    cross_q = to_heads(cross_q)
    *state, main_keys, main_values = attend(
        cross_q,
        [Rows(memory_near[0], rows), (memory_keys, memory_values), Rows(memory_near[1], rows)],
        None,
        *main_seen,
        None,
        None,
        False,
        (cross_key, cross_value),
    )
    state, memory_far = lax.optimization_barrier((state, memory_far))
    memory_far = [Rows([part] + others(part), cross_far) for part in memory_far]
    crossed, cross_lse, far_keys, far_values = attend(
        cross_q, memory_far, None, *far_seen, None, state, True, (cross_key, cross_value)
    )

    (
        outputs_rows,
        d_cross,
        d_crossed,
        adapter_grads,
    ) = feed_forward(
        core_index,
        crossed,
        to_rows(crossed),
        cross_outputs,
        first,
        cotangent,
        downs,
        down_biases,
        ups,
        adapter_up_bias,
        hidden_ins,
        hidden_outs,
    )
    d_crossed = to_heads(d_crossed)
    adapter_grads = dealt(after(adapter_grads, d_crossed))
    ups_count = adapter_up.shape[0]
    staged = shards % 4 == 0 and shards & (shards - 1) == 0 and 2 * ups_count % shards == 0
    if staged:
        plane, column = Ring(4, 1), Ring(shards // 4, 4)

    far_grads, query_state = attend_back(
        cross_q, d_crossed, crossed, far_keys, far_values, *far_seen[:2], cross_lse, far_seen[2],
        cross_key, cross_value, (0, cross_far, 2 * cross_far), cores,
    )
    far_grads, query_state, adapter_grads = lax.optimization_barrier(
        (far_grads, query_state, adapter_grads)
    )
    far_parts = [dealt(part) for part in far_grads]
    adapter_grads, bias_grads = add_up([adapter_grads], 2 * ups_count)
    if staged:
        adapter_arrived = plane.scatter(adapter_grads)
        adapter_kept = plane.cut(adapter_grads, 0)
    far_low = add_up(after(far_parts, adapter_grads))
    far_arrived = (shift(far_low[0], -2), shift(far_low[1], 2))
    query_state = after(query_state, far_low)
    near_grads, cross_q_grad = attend_back(
        cross_q, d_crossed, crossed, main_keys, main_values, *main_seen[:2], cross_lse,
        main_seen[2], cross_key, cross_value, (0, rows, 2 * rows, 3 * rows), cores, None, query_state, None,
        True,
    )
    far_arrived, near_grads, cross_q_grad = lax.optimization_barrier(
        (far_arrived, near_grads, cross_q_grad)
    )
    if staged:
        adapter_arrived, cross_q_grad = lax.optimization_barrier((adapter_arrived, cross_q_grad))
    grads_rows = to_rows(cross_q_grad)
    near_parts = [dealt(after(part, grads_rows)) for part in near_grads]
    d_tokens, d_attended = before_self(
        core_index, cross_q_grad, grads_rows, cross_queries, self_outputs, d_cross, first,
        first_scale,
    )
    d_attended = to_heads(d_attended)
    near_low = add_up(after([near_parts[0], near_parts[2]], d_attended))
    near_arrived = (shift(near_low[0], -1), shift(near_low[1], 1))
    outputs_other = others(after(outputs_rows, near_low))
    d_tokens_cols = to_heads(after(d_tokens, near_low))
    d_attended = after(d_attended, near_low)

    halo_grads, prefix_key_grad, prefix_value_grad, query_state = attend_back(
        query, d_attended, attended, self_keys, self_values, *halo_seen[:2], self_lse, halo_seen[2],
        self_key, self_value, (0, self_far, self_base), cores, prefix_rows,
    )
    halo_grads, query_state, near_arrived, outputs_other, d_tokens_cols = lax.optimization_barrier(
        (halo_grads, query_state, near_arrived, outputs_other, d_tokens_cols)
    )
    halo_parts = [dealt(part) for part in halo_grads]
    if staged:
        (adapter_grads,) = add_up([[adapter_kept] + after(adapter_arrived, query_state)])
        adapter_arrived = column.scatter(adapter_grads)
        adapter_kept = column.cut(adapter_grads, 0)
        halo_parts = after(halo_parts, adapter_grads)
    halo_low = add_up(halo_parts)
    halo_arrived = (shift(halo_low[0], -2), shift(halo_low[1], -1))
    pad = ((rows - cross_far, 0), (0, 0))
    back = ((0, rows - cross_far), (0, 0))
    near_own, near_arrived, far_arrived, outputs_rows, outputs_other = after(
        (near_parts[1], near_arrived, far_arrived, outputs_rows, outputs_other), halo_low
    )
    memory_sum = sum(
        [part.astype(f32) for part in near_own + list(near_arrived)],
        jnp.pad(far_arrived[0], pad).astype(f32) + jnp.pad(far_arrived[1], back).astype(f32),
    ).astype(bf16)
    outputs = in_order([outputs_rows] + outputs_other, 0)
    query_state = after(query_state, halo_low, memory_sum, outputs)
    ((here_grads,),) = attend_back(
        query, d_attended, attended, own_keys, own_values, *own_seen[:2], self_lse, own_seen[2],
        self_key, self_value, (0, rows), cores, None, query_state, self_query,
    )
    here_grads, halo_arrived, memory_sum = lax.optimization_barrier(
        (here_grads, halo_arrived, memory_sum)
    )
    if staged:
        adapter_arrived, here_grads = lax.optimization_barrier((adapter_arrived, here_grads))
    here_sum = over_cores(here_grads)
    memory_other = others(after(memory_sum, here_sum))
    kept = [adapter_kept] + adapter_arrived if staged else [adapter_grads]
    both = pack(kept, prefix_key_grad, prefix_value_grad, bias_grads)
    if staged:
        both_arrived = column.exchange([both] * column.size)
    grad_memory = beside(core_index, [memory_sum] + memory_other)
    token_sum = (
        d_tokens_cols.astype(f32)
        + here_sum
        + jnp.pad(halo_arrived[0], ((rows - self_far, 0), (0, 0))).astype(f32)
        + halo_arrived[1].astype(f32)
    ).astype(bf16)
    token_other = others(token_sum)
    grad_tokens = beside(core_index, [token_sum] + token_other)
    if staged:
        place = jnp.reshape(column.place, (1,)).astype(jnp.int32)
        (both,) = gather_rows(place, [both] + both_arrived, None)
        parts = [both] + plane.exchange([both] * plane.size)
        place = jnp.reshape(plane.place, (1,)).astype(jnp.int32)
    else:
        parts, place = [lax.psum(both, "seq")], core_index * 0
    parts = after(parts, grad_tokens)
    sizes = (prefix, cols, ups_count)
    prefix_k, prefix_v, grad_down, grad_down_bias, grad_up, grad_up_bias = gather_rows(place, parts, sizes)
    return (
        outputs,
        grad_tokens,
        grad_memory,
        prefix_k,
        prefix_v,
        grad_down,
        grad_down_bias[0],
        grad_up,
        grad_up_bias[0],
    )


def solution(mesh):
    in_specs = (
        P("seq", None),
        P("seq", None),
        P("seq", None),
        P(),
        P(),
        P(None, "head"),
        P(None, "head"),
        P(None, "head"),
        P("head", None),
        P(None, "head"),
        P(None, "head"),
        P(None, "head"),
        P("head", None),
        P(None, "head"),
        P("head", None),
        P(None, "head"),
        P(None, "head"),
        P(None, "head"),
        P("head"),
        P("head", None),
        P(),
    )
    out_specs = (
        P("seq", None),
        P("seq", None),
        P("seq", None),
        P(None, "head"),
        P(None, "head"),
        P(None, "head"),
        P("head"),
        P("head", None),
        P(),
    )
    return jax.shard_map(
        on_device, mesh=mesh, in_specs=in_specs, out_specs=out_specs, check_vma=False
    )
```

```python
import functools
from typing import NamedTuple

import jax
import jax.numpy as jnp
from jax import lax
from jax.experimental import pallas as pl
from jax.experimental.pallas import tpu as pltpu
from jax.sharding import PartitionSpec as P

HEAD_DIM = 64
MASKED = -1e30
LN2 = 0.6931471805599453
LOG2E = 1.4426950408889634
EPS = 1e-05
SEQ_MAX = 1792
DRIFT = 128
PAD = 128
BLOCK = 256
f32 = jnp.float32
bf16 = jnp.bfloat16


def dot(left, right):
    return jnp.dot(left, right, preferred_element_type=f32)


def dot_nt(left, right):
    return lax.dot_general(left, right, (((1,), (1,)), ((), ())), preferred_element_type=f32)


def dot_tn(left, right):
    return lax.dot_general(left, right, (((0,), (0,)), ((), ())), preferred_element_type=f32)


def split_rows(pair):
    zero = jnp.zeros((HEAD_DIM, pair.shape[1]), pair.dtype)
    return [
        jnp.concatenate([pair[:HEAD_DIM], zero], axis=0),
        jnp.concatenate([zero, pair[HEAD_DIM:]], axis=0),
    ]


def stack_lanes(pair):
    first = lax.broadcasted_iota(jnp.int32, pair.shape, 1) < HEAD_DIM
    zero = jnp.zeros_like(pair)
    return jnp.concatenate([jnp.where(first, pair, zero), jnp.where(first, zero, pair)], axis=0)


def over_range(low, high, body):
    def step(i, carry):
        body(pl.ds(pl.multiple_of(low + i * 128, 128), 128))
        return carry

    lax.fori_loop(0, pl.cdiv(high - low, 128), step, 0)


def over_tiles(info, segments, block, tile):
    def one_segment(segment, carry):
        first, count, low, high = (info[6 * segment + i, block] for i in range(4))

        def full(i, carry):
            tile(pl.multiple_of(first + i * BLOCK, 128), segment, False)
            return carry

        def edge(j, carry):
            i = jnp.where(j < low, j, j - low + high)
            tile(pl.multiple_of(first + i * BLOCK, 128), segment, True)
            return carry

        lax.fori_loop(low, high, full, 0)
        lax.fori_loop(0, low + count - high, edge, 0)
        return carry

    if segments == 1:
        one_segment(0, 0)
    else:
        lax.fori_loop(0, segments, one_segment, 0)


def span_of(info, segment):
    return info[6 * segment + 4, 0], info[6 * segment + 5, 0]


def in_spans(info, segments, test):
    result = test(*span_of(info, 0))
    for segment in range(1, segments):
        result = result | test(*span_of(info, segment))
    return result


def owned(info, segments, cores, before, length):
    owner = lax.rem(info[6 * segments, 0] + cores - before, cores)
    return pl.ds(pl.multiple_of(owner * length, length), length)


def allowed(row, start, end):
    place = row + lax.broadcasted_iota(jnp.int32, (BLOCK, start.shape[1]), 0)
    return (place >= start) & (place < end)


def pair_cols(head):
    return slice(head // 2 * 128, head // 2 * 128 + 128)


def head_rows(head):
    return slice(head * HEAD_DIM, head * HEAD_DIM + HEAD_DIM)


def attend_kernel(prefix, resume, last, segments, pieces, cores, info, *refs):
    refs = list(refs)
    q, start, end = refs[:3]
    del refs[:3]
    wk, wv = refs[:2]
    del refs[:2]
    parts = []
    for length, raw in pieces:
        count = cores if raw else 2
        parts.append(refs[:count])
        del refs[:count]
    if prefix:
        pk, pv = refs[:2]
        del refs[:2]
    if resume:
        top_in, total_in, acc_in = refs[:3]
        del refs[:3]
    outs = refs[: 2 if last else 3]
    del refs[: len(outs)]
    k, v = refs[:2]
    del refs[:2]
    vt = refs.pop(0)
    if last:
        out, lse = outs
        top, total, acc = refs[:3]
        del refs[:3]
    else:
        top, total, acc = outs
    block = pl.program_id(0)
    heads = q.shape[1] // HEAD_DIM

    def bring(piece, offset, length, sem):
        window = pl.ds(offset, length)
        return (
            pltpu.make_async_copy(piece[0], k.at[window, :], sem.at[0]),
            pltpu.make_async_copy(piece[1], v.at[window, :], sem.at[1]),
        )

    def project(piece, offset, length):
        def rows_at(row, size):
            window = pl.ds(offset + row, size)

            needed = lambda least, most: (offset + row < most) & (offset + row + size > least)

            @pl.when(in_spans(info, segments, needed))
            def _():
                source = pl.ds(row, size)
                depth = piece[0].shape[1]
                new_k, new_v = 0.0, 0.0
                for core, part in enumerate(piece):
                    some = owned(info, segments, cores, core, depth)
                    value = part[source, :]
                    new_k = new_k + dot(value, wk[some, :])
                    new_v = new_v + dot(value, wv[some, :])
                k[window, :] = new_k.astype(bf16)
                new_v = new_v.astype(bf16)
                v[window, :] = new_v
                vt[:, window] = new_v.T

        def step(i, carry):
            rows_at(pl.multiple_of(i * BLOCK, BLOCK), BLOCK)
            return carry

        full = length // BLOCK
        lax.fori_loop(0, full, step, 0)
        if length % BLOCK:
            rows_at(full * BLOCK, length % BLOCK)

    def turn_over(window):
        vt[:, window] = v[window, :].T

    @pl.when(block == 0)
    def _():
        offset, ready = 0, []
        for (length, raw), piece in zip(pieces, parts):
            if not raw:
                for copy in bring(piece, offset, length, refs[0]):
                    copy.start()
            offset += length
        rest = slice(offset, k.shape[0])
        k[rest, :] = jnp.zeros((k.shape[0] - offset, k.shape[1]), bf16)
        v[rest, :] = jnp.zeros((k.shape[0] - offset, k.shape[1]), bf16)
        vt[:, rest] = jnp.zeros((k.shape[1], k.shape[0] - offset), bf16)
        offset = 0
        for (length, raw), piece in zip(pieces, parts):
            if raw:
                project(piece, offset, length)
            offset += length
        offset = 0
        for (length, raw), piece in zip(pieces, parts):
            if not raw:
                for copy in bring(piece, offset, length, refs[0]):
                    copy.wait()
                for segment in range(segments):
                    least, most = span_of(info, segment)
                    over_range(
                        jnp.maximum(least, offset), jnp.minimum(most, offset + length), turn_over
                    )
            offset += length

    qs = []
    for pair in range(heads // 2):
        qs.extend(split_rows(q[:, pair * 128 : pair * 128 + 128].T))
    if resume:
        top[...] = top_in[...]
        total[...] = total_in[...]
        acc[...] = acc_in[...]
    elif prefix:
        there = lax.broadcasted_iota(jnp.int32, (32, BLOCK), 0) < prefix
        for head in range(heads):
            scores = jnp.where(there, dot(pk[:, pair_cols(head)], qs[head]), MASKED)
            peak = jnp.max(scores, axis=0, keepdims=True)
            weights = jnp.exp2(scores - peak)
            top[head : head + 1] = peak
            total[head : head + 1] = jnp.sum(weights, axis=0, keepdims=True)
            turned = pv[:, pair_cols(head)].T
            acc[head_rows(head)] = dot(turned[head_rows(head % 2)], weights.astype(bf16))
    else:
        top[...] = jnp.full(top.shape, MASKED, f32)
        total[...] = jnp.zeros(total.shape, f32)
        acc[...] = jnp.zeros(acc.shape, f32)

    def tile(row, segment, edge):
        window = pl.ds(row, BLOCK)
        if edge:
            seen = pl.ds(segment, 1)
            open_ = allowed(row, start[seen, :], end[seen, :])
        scores = [dot(k[window, pair_cols(head)], qs[head]) for head in range(heads)]
        for head in range(heads):
            score = scores[head]
            if edge:
                score = jnp.where(open_, score, MASKED)
            old = top[head : head + 1]
            peak = jnp.maximum(old, jnp.max(score, axis=0, keepdims=True))
            weights = jnp.exp2(score - peak)
            scale = jnp.exp2(old - peak)
            top[head : head + 1] = peak
            total[head : head + 1] = total[head : head + 1] * scale + jnp.sum(
                weights, axis=0, keepdims=True
            )
            acc[head_rows(head)] = acc[head_rows(head)] * scale + dot(
                vt[head_rows(head), window], weights.astype(bf16)
            )

    over_tiles(info, segments, block, tile)
    if last:
        for pair in range(heads // 2):
            parts = [
                acc[head_rows(head)] * (1.0 / total[head : head + 1])
                for head in (2 * pair, 2 * pair + 1)
            ]
            out[:, pair * 128 : pair * 128 + 128] = (
                jnp.concatenate(parts, axis=0).T.astype(bf16)
            )
        lse[...] = top[...] + jnp.log2(total[...])


def kernel_params():
    return pltpu.CompilerParams(
        dimension_semantics=("arbitrary",), vmem_limit_bytes=60 << 20
    )


class Rows(NamedTuple):
    parts: list
    length: int


def attend(query, keys, weights, start, end, info, prefix=None, state=None, last=True):
    rows, cols = query.shape
    heads = cols // HEAD_DIM
    by_rows = pl.BlockSpec((BLOCK, cols), lambda b, info: (b, 0))
    by_lanes = lambda count: pl.BlockSpec((count, BLOCK), lambda b, info: (0, b))
    whole = lambda count, wide=cols: pl.BlockSpec((count, wide), lambda b, info: (0, 0))
    segments = start.shape[0]
    operands = [query, start, end]
    specs = [by_rows, by_lanes(segments), by_lanes(segments)]
    cores = 1
    pieces = tuple(
        (piece.length, True) if isinstance(piece, Rows) else (piece[0].shape[0], False)
        for piece in keys
    )
    window = sum(length for length, raw in pieces) + PAD
    operands += list(weights)
    specs += [whole(weights[0].shape[0])] * 2
    for (length, raw), piece in zip(pieces, keys):
        if raw:
            cores = len(piece.parts)
            operands += list(piece.parts)
            specs += [whole(length, part.shape[1]) for part in piece.parts]
        else:
            operands += list(piece)
            specs += [pl.BlockSpec(memory_space=pl.ANY)] * 2
    if prefix is not None:
        operands += [prefix[0], prefix[1]]
        specs += [whole(32), whole(32)]
    state_specs = [by_lanes(heads), by_lanes(heads), by_lanes(cols)]
    if state is not None:
        operands += list(state)
        specs += state_specs
    shape = jax.ShapeDtypeStruct
    scratch = [pltpu.VMEM((cols, window), bf16)]
    if last:
        outs = [shape((rows, cols), bf16), shape((heads, rows), f32)]
        out_specs = [by_rows, by_lanes(heads)]
        scratch += [pltpu.VMEM((n, BLOCK), f32) for n in (heads, heads, cols)]
    else:
        outs = [shape((n, rows), f32) for n in (heads, heads, cols)]
        out_specs = list(state_specs)
    outs += [shape((window, cols), bf16)] * 2
    out_specs += [whole(window)] * 2
    scratch.append(pltpu.SemaphoreType.DMA((2,)))
    return pl.pallas_call(
        functools.partial(
            attend_kernel, 0 if prefix is None else prefix[2], state is not None, last, segments,
            pieces, cores,
        ),
        out_shape=tuple(outs),
        grid_spec=pltpu.PrefetchScalarGridSpec(
            num_scalar_prefetch=1,
            grid=(rows // BLOCK,),
            in_specs=specs,
            out_specs=tuple(out_specs),
            scratch_shapes=scratch,
        ),
        compiler_params=kernel_params(),
    )(info, *operands)


def attend_back_kernel(
    prefix, resume, own, final, lengths, cuts, cores, segments, info, *refs
):
    refs = list(refs)
    q, d_out, out, start, end, lse, wk, wv = refs[:8]
    del refs[:8]
    sources = [refs[2 * i : 2 * i + 2] for i in range(len(lengths))]
    del refs[: 2 * len(lengths)]
    if prefix:
        pk, pv = refs[:2]
        del refs[:2]
    if resume:
        dq_in = refs.pop(0)
    if own is not None:
        wq = refs.pop(0)
    pieces = len(cuts)
    grads = [refs[i * cores : i * cores + cores] for i in range(pieces)]
    del refs[: pieces * cores]
    if prefix:
        dpk, dpv = refs[:2]
        del refs[:2]
    if own is None:
        dq_out = refs.pop(0)
    k, v, kt, dk, dv, dq, sem = refs[:7]
    if own is not None:
        dq_low = refs[7]
    block = pl.program_id(0)
    heads = q.shape[1] // HEAD_DIM
    pairs = heads // 2

    @pl.when(block == 0)
    def _():
        copies, offset = [], 0
        for i, (length, source) in enumerate(zip(lengths, sources)):
            for j, (there, here) in enumerate(zip(source, (k, v))):
                copies.append(
                    pltpu.make_async_copy(
                        there.at[pl.ds(0, length), :],
                        here.at[pl.ds(offset, length), :],
                        sem.at[2 * i + j],
                    )
                )
            offset += length
        for copy in copies:
            copy.start()
        if offset < k.shape[0]:
            rest = slice(offset, k.shape[0])
            k[rest, :] = jnp.zeros((k.shape[0] - offset, k.shape[1]), bf16)
            v[rest, :] = jnp.zeros((k.shape[0] - offset, k.shape[1]), bf16)
        if prefix:
            dpk[...] = jnp.zeros(dpk.shape, f32)
            dpv[...] = jnp.zeros(dpv.shape, f32)

        def clear(window):
            dk[window, :] = jnp.zeros((128, dk.shape[1]), f32)
            dv[window, :] = jnp.zeros((128, dv.shape[1]), f32)

        def turn_over(window):
            kt[:, window] = k[window, :].T

        for segment in range(segments):
            over_range(*span_of(info, segment), clear)
        for copy in copies:
            copy.wait()
        for segment in range(segments):
            over_range(*span_of(info, segment), turn_over)

    qs, ds, delta, q_stack, d_stack = [], [], [], [], []
    for pair in range(pairs):
        cols = slice(pair * 128, pair * 128 + 128)
        q_pair, d_pair = q[:, cols], d_out[:, cols]
        qs.extend(split_rows(q_pair.T))
        ds.extend(split_rows(d_pair.T))
        both = (d_pair.astype(f32) * out[:, cols].astype(f32)).T
        delta.append(jnp.sum(both[:HEAD_DIM], axis=0, keepdims=True))
        delta.append(jnp.sum(both[HEAD_DIM:], axis=0, keepdims=True))
        q_stack.append(stack_lanes(q_pair))
        d_stack.append(stack_lanes(d_pair))
    if resume:
        dq[...] = dq_in[...]
    else:
        dq[...] = jnp.zeros(dq.shape, f32)
    if prefix:
        there = lax.broadcasted_iota(jnp.int32, (32, BLOCK), 0) < prefix
        for pair in range(pairs):
            cols = slice(pair * 128, pair * 128 + 128)
            turned = pk[:, cols].T
            ws, gs = [], []
            for head in (2 * pair, 2 * pair + 1):
                scores = dot(pk[:, cols], qs[head])
                weights = jnp.where(there, jnp.exp2(scores - lse[head : head + 1]), 0.0)
                grad = (weights * (dot(pv[:, cols], ds[head]) - delta[head])).astype(bf16)
                dq[head_rows(head)] += dot(turned[head_rows(head % 2)], grad)
                ws.append(weights.astype(bf16))
                gs.append(grad)
            dpv[:, cols] += dot(jnp.concatenate(ws, axis=1), d_stack[pair])
            dpk[:, cols] += dot(jnp.concatenate(gs, axis=1), q_stack[pair]) * LN2

    def tile(row, segment, edge):
        window = pl.ds(row, BLOCK)
        if edge:
            seen = pl.ds(segment, 1)
            open_ = allowed(row, start[seen, :], end[seen, :])
        scores = [dot(k[window, pair_cols(head)], qs[head]) for head in range(heads)]
        inner = [dot(v[window, pair_cols(head)], ds[head]) for head in range(heads)]
        for pair in range(pairs):
            cols = slice(pair * 128, pair * 128 + 128)
            ws, gs = [], []
            for head in (2 * pair, 2 * pair + 1):
                weights = jnp.exp2(scores[head] - lse[head : head + 1])
                if edge:
                    weights = jnp.where(open_, weights, 0.0)
                grad = (weights * (inner[head] - delta[head])).astype(bf16)
                dq[head_rows(head)] += dot(kt[head_rows(head), window], grad)
                ws.append(weights.astype(bf16))
                gs.append(grad)
            dv[window, cols] += dot(jnp.concatenate(ws, axis=1), d_stack[pair])
            dk[window, cols] += dot(jnp.concatenate(gs, axis=1), q_stack[pair])

    over_tiles(info, segments, block, tile)
    if own is None and final:
        dq_out[...] = (dq[...] * 0.125).T.astype(bf16)
    elif own is None:
        dq_out[...] = dq[...]
    else:
        dq_low[pl.ds(pl.multiple_of(block * BLOCK, BLOCK), BLOCK), :] = (
            (dq[...] * 0.125).T.astype(bf16)
        )

    @pl.when(block == pl.num_programs(0) - 1)
    def _():
        def project(row, size, piece, offset):
            window = pl.ds(row, size)
            target = pl.ds(offset, size)
            touched = in_spans(
                info, segments, lambda least, most: (row < most) & (row + size > least)
            )
            width = grads[piece][0].shape[1]

            @pl.when(touched)
            def _():
                place = row + lax.broadcasted_iota(jnp.int32, (size, dk.shape[1]), 0)
                there = in_spans(
                    info, segments, lambda least, most: (place >= least) & (place < most)
                )
                dk_low = jnp.where(there, dk[window, :] * LN2, 0.0).astype(bf16)
                dv_low = jnp.where(there, dv[window, :], 0.0).astype(bf16)
                for core in range(cores):
                    part = owned(info, segments, cores, core, width)
                    value = dot_nt(dk_low, wk[part, :]) + dot_nt(dv_low, wv[part, :])
                    if own == piece:
                        value += dot_nt(dq_low[target, :], wq[part, :])
                    grads[piece][core][target, :] = value.astype(bf16)

            @pl.when(jnp.logical_not(touched))
            def _():
                for core in range(cores):
                    value = jnp.zeros((size, width), f32)
                    if own == piece:
                        part = owned(info, segments, cores, core, width)
                        value = dot_nt(dq_low[target, :], wq[part, :])
                    grads[piece][core][target, :] = value.astype(bf16)

        for piece, (begin, length) in enumerate(cuts):
            whole = length // BLOCK

            def step(i, carry, piece=piece, begin=begin):
                offset = pl.multiple_of(i * BLOCK, BLOCK)
                project(pl.multiple_of(begin + offset, 128), BLOCK, piece, offset)
                return carry

            lax.fori_loop(0, whole, step, 0)
            rest = length - whole * BLOCK
            if rest:
                project(begin + whole * BLOCK, rest, piece, whole * BLOCK)


def attend_back(
    query, d_out, out, sources, weights, start, end, info, lse, cuts, cores, prefix=None, own=None,
    state=None, final=False, pad=0,
):
    rows, cols = query.shape
    lengths = tuple(length for _, _, length in sources)
    window = sum(lengths) + pad
    width = weights[0].shape[0]
    heads = cols // HEAD_DIM
    segments = start.shape[0]
    by_rows = pl.BlockSpec((BLOCK, cols), lambda b, info: (b, 0))
    by_lanes = lambda count: pl.BlockSpec((count, BLOCK), lambda b, info: (0, b))
    whole = lambda count, wide=cols: pl.BlockSpec((count, wide), lambda b, info: (0, 0))
    operands = [query, d_out, out, start, end, lse] + list(weights[:2])
    specs = [by_rows] * 3 + [by_lanes(segments)] * 2 + [by_lanes(heads)] + [whole(width)] * 2
    for keys, values, _ in sources:
        operands += [keys, values]
        specs += [pl.BlockSpec(memory_space=pl.ANY)] * 2
    if prefix is not None:
        operands += [prefix[0], prefix[1]]
        specs += [whole(32), whole(32)]
    if state is not None:
        operands.append(state)
        specs.append(by_lanes(cols))
    if own is not None:
        operands.append(weights[2])
        specs.append(whole(width))
    shape = jax.ShapeDtypeStruct
    outs, out_specs = [], []
    for _, length in cuts:
        outs += [shape((length, width // cores), bf16)] * cores
        out_specs += [whole(length, width // cores)] * cores
    if prefix is not None:
        outs += [shape((32, cols), f32)] * 2
        out_specs += [whole(32)] * 2
    if own is None and final:
        outs.append(shape((rows, cols), bf16))
        out_specs.append(by_rows)
    elif own is None:
        outs.append(shape((cols, rows), f32))
        out_specs.append(by_lanes(cols))
    scratch = [
        pltpu.VMEM((window, cols), bf16),
        pltpu.VMEM((window, cols), bf16),
        pltpu.VMEM((cols, window), bf16),
        pltpu.VMEM((window, cols), f32),
        pltpu.VMEM((window, cols), f32),
        pltpu.VMEM((cols, BLOCK), f32),
        pltpu.SemaphoreType.DMA((2 * len(sources),)),
    ]
    if own is not None:
        scratch.append(pltpu.VMEM((rows, cols), bf16))
    result = pl.pallas_call(
        functools.partial(
            attend_back_kernel, 0 if prefix is None else prefix[2], state is not None, own, final,
            lengths, tuple(cuts), cores, segments,
        ),
        out_shape=tuple(outs),
        grid_spec=pltpu.PrefetchScalarGridSpec(
            num_scalar_prefetch=1,
            grid=(rows // BLOCK,),
            in_specs=specs,
            out_specs=tuple(out_specs),
            scratch_shapes=scratch,
        ),
        compiler_params=kernel_params(),
    )(info, *operands)
    pieces = [list(result[i * cores : i * cores + cores]) for i in range(len(cuts))]
    return pieces, *result[len(cuts) * cores :]


class Span(NamedTuple):
    segments: tuple
    causal: bool = True


def spans_kernel(spans, total, rows, tgt, mem, at, *refs):
    here, core = at[0], at[1]
    place = here + lax.broadcasted_iota(jnp.int32, (1, rows), 1)

    def one(j, carry):
        begin, mem_begin, start, mem_start, mem_end = carry
        end, mem_stop = begin + tgt[j], mem_begin + mem[j]
        past = place >= end
        start = jnp.where(past, end, start)
        mem_start = jnp.where(past, mem_stop, mem_start)
        mem_end = jnp.where(place >= begin, mem_stop, mem_end)
        return end, mem_stop, start, mem_start, mem_end

    zero = jnp.zeros((1, rows), jnp.int32)
    begin, _, start, mem_start, mem_end = lax.fori_loop(
        0, tgt.shape[0], one, (0, 0, zero, zero, zero)
    )
    mem_end = jnp.where(place >= begin, total, mem_end)
    blocks = rows // BLOCK

    def least(value, block):
        part = value[:, block * BLOCK : block * BLOCK + BLOCK].astype(f32)
        return jnp.min(part).astype(jnp.int32)

    def most(value, block):
        part = value[:, block * BLOCK : block * BLOCK + BLOCK].astype(f32)
        return jnp.max(part).astype(jnp.int32)

    ends = [
        [(least(value, b), most(value, b)) for b in range(blocks)]
        for value in (start - here, mem_start - here, mem_end - here)
    ]
    for i, span in enumerate(spans):
        starts_out, ends_out, info = refs[3 * i : 3 * i + 3]
        for segment, (base, low, high) in enumerate(span.segments):
            clip = lambda value: jnp.clip(value + base, low, high)
            if span.causal:
                lows, highs = start - here, place - here + 1
                corners = [(ends[0][b], (b * BLOCK + 1, b * BLOCK + BLOCK)) for b in range(blocks)]
            else:
                lows, highs = mem_start - here, mem_end - here
                corners = [(ends[1][b], ends[2][b]) for b in range(blocks)]
            starts_out[segment : segment + 1, :] = clip(lows)
            ends_out[segment : segment + 1, :] = clip(highs)
            lowest, highest = 1 << 20, 0
            for b, ((s0, s1), (e0, e1)) in enumerate(corners):
                s0, s1, e0, e1 = clip(s0), clip(s1), clip(e0), clip(e1)
                some = e1 > s0
                first = jnp.where(some, s0 // 128 * 128, 0)
                count = jnp.where(some, (e1 - first + BLOCK - 1) // BLOCK, 0)
                from_ = jnp.clip((s1 - first + BLOCK - 1) // BLOCK, 0, count)
                to = jnp.clip((e0 - first) // BLOCK, from_, count)
                for row, value in enumerate((first, count, from_, to)):
                    info[6 * segment + row, b] = value
                lowest = jnp.where(some, jnp.minimum(lowest, first), lowest)
                highest = jnp.where(some, jnp.maximum(highest, first + count * BLOCK), highest)
            for b in range(blocks):
                info[6 * segment + 4, b] = jnp.minimum(lowest, highest)
                info[6 * segment + 5, b] = highest
        for b in range(blocks):
            info[6 * len(span.segments), b] = core


def see(spans, total, rows, tgt, mem, at):
    outs, specs = [], []
    for span in spans:
        count = len(span.segments)
        outs += [jax.ShapeDtypeStruct((count, rows), jnp.int32)] * 2
        outs.append(jax.ShapeDtypeStruct((6 * count + 1, rows // BLOCK), jnp.int32))
        specs += [pl.BlockSpec((count, rows), lambda i, *scalars: (0, 0))] * 2
        specs.append(pl.BlockSpec(memory_space=pltpu.SMEM))
    result = pl.pallas_call(
        functools.partial(spans_kernel, spans, total, rows),
        out_shape=tuple(outs),
        grid_spec=pltpu.PrefetchScalarGridSpec(
            num_scalar_prefetch=3, grid=(1,), in_specs=[], out_specs=tuple(specs)
        ),
    )(tgt, mem, at)
    return [result[3 * i : 3 * i + 3] for i in range(len(spans))]


def norm_parts(value):
    center = value - jnp.mean(value, axis=-1, keepdims=True)
    scale = lax.rsqrt(jnp.mean(center * center, axis=-1, keepdims=True) + EPS)
    return center * scale, scale


def norm_back(normal, scale, grad):
    return scale * (
        grad
        - jnp.mean(grad, axis=-1, keepdims=True)
        - normal * jnp.mean(grad * normal, axis=-1, keepdims=True)
    )


def gelu_pair(value):
    size = jnp.abs(value)
    bell = jnp.exp(-0.5 * value * value)
    under = 1.0 + (0.3275911 * 0.7071067811865476) * size
    t = pl.reciprocal(under, approx=True)
    t = t * (2.0 - under * t)
    poly = ((((1.061405429 * t - 1.453152027) * t + 1.421413741) * t - 0.284496736) * t + 0.254829592) * t
    tail = 0.5 * poly * bell
    cdf = jnp.where(value >= 0, 1.0 - tail, tail)
    return value * cdf, cdf + value * (0.3989422804014327 * bell)


def ffn_kernel(cores, chunk, core, *refs):
    refs = list(refs)

    def take(count):
        taken = refs[:count]
        del refs[:count]
        return taken

    crossed = take(cores)
    cross_outs = take(cores)
    first, cot = take(2)
    downs = take(cores)
    biases = take(cores)
    ups = take(cores)
    (up_bias,) = take(1)
    hins, houts = take(2)
    cross_outs, downs, ups = ([ref.at[0] for ref in part] for part in (cross_outs, downs, ups))
    out, d_cross = take(2)
    d_crossed = take(cores)
    adapter_grads = take(cores)
    hin, hout, in_sem, out_sem, slope, bufs0, bufs1, branch, second, second_low, adapted, down_slope, low = refs
    per = hins.shape[2] // chunk
    count = per * cores
    adapt = downs[0].shape[1]

    def copies(j):
        c, i = divmod(j, per)
        part = pl.ds(i * chunk, chunk)
        return (
            pltpu.make_async_copy(hins.at[c, :, part], hin.at[j], in_sem.at[j]),
            pltpu.make_async_copy(houts.at[c, part, :], hout.at[j], out_sem.at[j]),
        )

    for j in range(count):
        for copy in copies(j):
            copy.start()
    total = first[...]
    for value, weight in zip(crossed, cross_outs):
        total = total + dot(value[...], weight[...])
    normal, scale2 = norm_parts(total)
    second[...] = normal
    second_low[...] = normal.astype(bf16)

    wide = 4.0 * up_bias[...]
    acc = jnp.zeros(branch.shape, f32)
    for c in range(cores):
        part = slice(c * adapt, (c + 1) * adapt)
        value, grad = gelu_pair(dot(second_low[...], downs[c][...]) + biases[c][...])
        adapted[:, part] = value.astype(bf16)
        down_slope[:, part] = grad
        acc = acc + dot(adapted[:, part], ups[c][...])
    branch[...] = 4.0 * acc + wide

    for j in range(count):
        for copy in copies(j):
            copy.wait()
    bufs0[...] = dot(second_low[...], hin[0])

    def forward(j, now, later):
        later[...] = dot(second_low[...], hin[jnp.minimum(j + 1, count - 1)])
        value, grad = gelu_pair(now[...])
        slope[j] = grad.astype(bf16)
        branch[...] += dot(value.astype(bf16), hout[j])

    def forward_two(i, _):
        forward(2 * i, bufs0, bufs1)
        forward(2 * i + 1, bufs1, bufs0)
        return 0

    lax.fori_loop(0, count // 2, forward_two, 0)
    normal, scale = norm_parts(second[...] + branch[...])
    out[...] = normal.astype(bf16)
    d_third = norm_back(normal, scale, cot[...].astype(f32))
    branch[...] = d_third
    low[...] = d_third.astype(bf16)
    up_sum = 4.0 * jnp.sum(low[...].astype(f32), axis=0, keepdims=True)
    line = lax.broadcasted_iota(jnp.int32, (16, up_sum.shape[1]), 0)

    def backward(j):
        value = (slope[j].astype(f32) * dot_nt(low[...], hout[j])).astype(bf16)
        branch[...] += dot_nt(value, hin[j])

    def backward_two(i, _):
        backward(2 * i)
        backward(2 * i + 1)
        return 0

    lax.fori_loop(0, count // 2, backward_two, 0)
    total = branch[...]
    for c in range(cores):
        part = slice(c * adapt, (c + 1) * adapt)
        value = (down_slope[:, part] * (4.0 * dot_nt(low[...], ups[c][...]))).astype(bf16)
        total = total + dot_nt(value, downs[c][...])
        adapter_grads[c][adapt : 2 * adapt, :] = dot_tn(value, second_low[...]).astype(bf16)
        adapter_grads[c][:adapt, :] = (4.0 * dot_tn(adapted[:, part], low[...])).astype(bf16)
        down_sum = jnp.sum(value.astype(f32), axis=0, keepdims=True)
        down_sum = jnp.concatenate(
            [down_sum, jnp.zeros((1, up_sum.shape[1] - adapt), f32)], axis=1
        )
        biases_low = jnp.where(line == 0, up_sum, jnp.where(line == 1, down_sum, 0.0))
        adapter_grads[c][2 * adapt :, :] = biases_low.astype(bf16)
    d_second = norm_back(second[...], scale2, total)
    d_cross[...] = d_second
    for result, weight in zip(d_crossed, cross_outs):
        result[...] = dot_nt(d_second.astype(bf16), weight[...]).astype(bf16)


def at_core(cores, rows, width):
    return pl.BlockSpec((rows, width), lambda i, core: (core[0], 0))


def down_from_core(cores, shape):
    def spec(k):
        return pl.BlockSpec(
            (1,) + shape, lambda i, core: (lax.rem(core[0] + cores - k, cores), 0, 0)
        )

    return [spec(k) for k in range(cores)]


def one_step(kernel, core, operands, specs, outs, scratch):
    whole = lambda shape: pl.BlockSpec(shape, lambda i, core: (0,) * len(shape))
    specs = [whole(op.shape) if spec is None else spec for op, spec in zip(operands, specs)]
    return pl.pallas_call(
        kernel,
        out_shape=tuple(outs),
        grid_spec=pltpu.PrefetchScalarGridSpec(
            num_scalar_prefetch=1,
            grid=(1,),
            in_specs=specs,
            out_specs=tuple(whole(out.shape) for out in outs),
            scratch_shapes=scratch,
        ),
        compiler_params=kernel_params(),
    )(core, *operands)


def feed_forward(core, crossed, crossed_others, cross_outs, first, cot, downs, biases, ups, up_bias, hins, houts):
    rows, width = first.shape
    cores, _, hidden = hins.shape
    adapt = downs.shape[2]
    heads = crossed.shape[1]
    chunk = min(512, hidden)
    count = cores * hidden // chunk
    hbm = pl.BlockSpec(memory_space=pl.ANY)
    operands = [crossed] + list(crossed_others)
    specs = [at_core(cores, rows, heads)] + [None] * (cores - 1)
    operands += [cross_outs] * cores + [first, cot]
    specs += down_from_core(cores, cross_outs.shape[1:]) + [None, at_core(cores, rows, width)]
    operands += [downs] * cores + [bias[None] for bias in biases] + [ups] * cores + [up_bias[None]]
    specs += down_from_core(cores, downs.shape[1:]) + [None] * cores
    specs += down_from_core(cores, ups.shape[1:]) + [None]
    operands += [hins, houts]
    specs += [hbm, hbm]
    shape = jax.ShapeDtypeStruct
    outs = (
        [shape((rows, width), bf16), shape((rows, width), f32)]
        + [shape((rows, heads), bf16)] * cores
        + [shape((2 * adapt + 16, width), bf16)] * cores
    )
    scratch = [
        pltpu.VMEM((count, width, chunk), bf16),
        pltpu.VMEM((count, chunk, width), bf16),
        pltpu.SemaphoreType.DMA((count,)),
        pltpu.SemaphoreType.DMA((count,)),
        pltpu.VMEM((count, rows, chunk), bf16),
        pltpu.VMEM((rows, chunk), f32),
        pltpu.VMEM((rows, chunk), f32),
        pltpu.VMEM((rows, width), f32),
        pltpu.VMEM((rows, width), f32),
        pltpu.VMEM((rows, width), bf16),
        pltpu.VMEM((rows, adapt * cores), bf16),
        pltpu.VMEM((rows, adapt * cores), f32),
        pltpu.VMEM((rows, width), bf16),
    ]
    result = one_step(
        functools.partial(ffn_kernel, cores, chunk), core, operands, specs, outs, scratch
    )
    at = 2 + cores
    return result[0], result[1], list(result[2:at]), list(result[at:])


def after_self_kernel(cores, core, *refs):
    refs = list(refs)
    attended, refs = refs[:cores], refs[cores:]
    outputs, refs = refs[:cores], refs[cores:]
    queries, refs = refs[:cores], refs[cores:]
    tokens, first, scale = refs[:3]
    total = tokens[...].astype(f32)
    for value, weight in zip(attended, outputs):
        total = total + dot(value[...], weight[0])
    normal, inverse = norm_parts(total)
    first[...] = normal
    scale[...] = inverse
    low = normal.astype(bf16)
    for result, weight in zip(refs[3:], queries):
        result[...] = (dot(low, weight[0]) * (0.125 * LOG2E)).astype(bf16)


def after_self(core, attended, attended_others, outputs, queries, tokens):
    cores, heads, width = outputs.shape
    rows = tokens.shape[0] // cores
    operands = [attended] + list(attended_others) + [outputs] * cores + [queries] * cores + [tokens]
    specs = [at_core(cores, rows, heads)] + [None] * (cores - 1)
    specs += down_from_core(cores, outputs.shape[1:]) + down_from_core(cores, queries.shape[1:])
    specs += [at_core(cores, rows, width)]
    shape = jax.ShapeDtypeStruct
    outs = [shape((rows, width), f32), shape((rows, 1), f32)] + [shape((rows, heads), bf16)] * cores
    result = one_step(
        functools.partial(after_self_kernel, cores), core, operands, specs, outs, []
    )
    return result[0], result[1], list(result[2:])


def before_self_kernel(cores, core, *refs):
    refs = list(refs)
    grads, refs = refs[:cores], refs[cores:]
    queries, refs = refs[:cores], refs[cores:]
    outputs, refs = refs[:cores], refs[cores:]
    d_cross, first, scale, kept = refs[:4]
    sent, refs = refs[4 : 3 + cores], refs[3 + cores :]
    d_attended, d_tokens = refs[:cores], refs[cores]
    total = d_cross[...]
    for value, weight in zip(grads, queries):
        total = total + dot_nt(value[...], weight[0])
    total = norm_back(first[...], scale[...], total)
    d_tokens[...] = total
    low = total.astype(bf16)
    for result, weight in zip(d_attended, outputs):
        result[...] = dot_nt(low, weight[0]).astype(bf16)
    width = kept.shape[1]
    for k, result in enumerate([kept] + sent):
        owner = lax.rem(core[0] + cores - k, cores)
        part = pl.ds(pl.multiple_of(owner * width, width), width)
        result[...] = d_tokens[:, part].astype(result.dtype)


def before_self(core, grads, grads_others, queries, outputs, d_cross, first, scale):
    cores, heads, width = outputs.shape
    rows = first.shape[0]
    operands = [grads] + list(grads_others) + [queries] * cores + [outputs] * cores
    operands += [d_cross, first, scale]
    specs = [at_core(cores, rows, heads)] + [None] * (cores - 1)
    specs += down_from_core(cores, queries.shape[1:]) + down_from_core(cores, outputs.shape[1:])
    specs += [None] * 3
    shape = jax.ShapeDtypeStruct
    outs = [shape((rows, width // cores), f32)] + [shape((rows, width // cores), bf16)] * (cores - 1)
    outs += [shape((rows, heads), bf16)] * cores
    result = one_step(
        functools.partial(before_self_kernel, cores), core, operands, specs, outs,
        [pltpu.VMEM((rows, width), f32)],
    )
    return list(result[:cores]), list(result[cores:])


def beside_kernel(core, *refs):
    which = pl.program_id(0)
    for k, part in enumerate(refs[:-1]):

        @pl.when(which == k)
        def _(part=part):
            refs[-1][...] = part[...].astype(f32)


def beside(core, parts):
    rows, width = parts[0].shape
    cores = len(parts)
    count = 2

    def part_spec(k):
        def place(which, block, core):
            return (jnp.where(which == k, block, jnp.where(which < k, 0, count - 1)), 0)

        return pl.BlockSpec((rows // count, width), place)

    return pl.pallas_call(
        beside_kernel,
        out_shape=jax.ShapeDtypeStruct((rows, cores * width), f32),
        grid_spec=pltpu.PrefetchScalarGridSpec(
            num_scalar_prefetch=1,
            grid=(cores, count),
            in_specs=[part_spec(k) for k in range(cores)],
            out_specs=pl.BlockSpec(
                (rows // count, width),
                lambda which, block, core: (block, lax.rem(core[0] + cores - which, cores)),
            ),
        ),
    )(core, *parts)


def add_kernel(count, each, cut, *refs):
    for i in range(count):
        total = refs[i * each][...].astype(f32)
        for ref in refs[i * each + 1 : i * each + each]:
            total = total + ref[...].astype(f32)
        if cut is None:
            refs[count * each + i][...] = total.astype(bf16)
        else:
            refs[each][...] = total[:cut].astype(bf16)
            refs[each + 1][...] = total[cut:]


def add_up(lists, cut=None):
    each = len(lists[0])
    shape = jax.ShapeDtypeStruct
    outs = [shape(parts[0].shape, bf16) for parts in lists]
    if cut is not None:
        rows, width = lists[0][0].shape
        outs = [shape((cut, width), bf16), shape((rows - cut, width), f32)]
    return pl.pallas_call(
        functools.partial(add_kernel, len(lists), each, cut),
        out_shape=tuple(outs),
        compiler_params=pltpu.CompilerParams(vmem_limit_bytes=60 << 20),
    )(*[part for parts in lists for part in parts])


SMALL = 32


def pack_kernel(count, *refs):
    parts, refs = refs[:count], refs[count:]
    keys, values, biases, out = refs
    rows = parts[0].shape[0]
    total = parts[0][...].astype(f32)
    for part in parts[1:]:
        total = total + part[...].astype(f32)
    out[:rows, :] = total.astype(bf16)
    zero = jnp.zeros((SMALL, out.shape[1] - 2 * keys.shape[1]), f32)
    beside_ = [keys[...], values[...]] + ([zero] if zero.shape[1] else [])
    line = lax.broadcasted_iota(jnp.int32, (SMALL, out.shape[1]), 0)
    rest = jnp.where(line == SMALL - 2, biases[0:1], biases[1:2])
    small = jnp.where(line < SMALL - 2, jnp.concatenate(beside_, axis=1), rest)
    out[rows:, :] = small.astype(bf16)


def pack(parts, keys, values, biases):
    rows, width = parts[0].shape
    return pl.pallas_call(
        functools.partial(pack_kernel, len(parts)),
        out_shape=jax.ShapeDtypeStruct((rows + SMALL, width), bf16),
    )(*parts, keys, values, biases)


def gather_kernel(count, rows, last, place, *refs):
    parts, refs = refs[:count], refs[count:]
    total = parts[0][rows:, :].astype(f32)
    for part in parts[1:]:
        total = total + part[rows:, :].astype(f32)
    if last is None:
        (out,) = refs
        joined = out
        out[count * rows :, :] = total.astype(bf16)
    else:
        keys, values, down, down_bias, up, up_bias, joined = refs
        prefix, cols = keys.shape
        keys[...] = total[:prefix, :cols]
        values[...] = total[:prefix, cols : 2 * cols]
        up_bias[...] = total[SMALL - 2 : SMALL - 1]
        down_bias[...] = total[SMALL - 1 : SMALL, : down_bias.shape[1]]
    for k, part in enumerate(parts):
        owner = jnp.bitwise_xor(place[0], k)
        joined[pl.ds(pl.multiple_of(owner * rows, 16), rows), :] = part[:rows, :]
    if last is not None:
        up[...] = joined[: up.shape[0], :].astype(f32)
        down[...] = joined[up.shape[0] :, :].astype(f32).T


def gather_rows(place, parts, last):
    count = len(parts)
    length, width = parts[0].shape
    rows = length - SMALL
    shape = jax.ShapeDtypeStruct
    if last is None:
        outs, scratch = [shape((count * rows + SMALL, width), bf16)], []
    else:
        prefix, cols, adapt = last
        outs = [
            shape((prefix, cols), f32),
            shape((prefix, cols), f32),
            shape((width, adapt), f32),
            shape((1, adapt), f32),
            shape((adapt, width), f32),
            shape((1, width), f32),
        ]
        scratch = [pltpu.VMEM((count * rows, width), bf16)]
    return one_step(
        functools.partial(gather_kernel, count, rows, last),
        place,
        parts,
        [None] * count,
        outs,
        scratch,
    )


def stack_kernel(cores, core, *refs):
    out = refs[-1]
    rows = refs[0].shape[0]
    for k, part in enumerate(refs[:-1]):
        owner = lax.rem(core[0] + cores - k, cores)
        out[pl.ds(pl.multiple_of(owner * rows, 16), rows), :] = part[...].astype(out.dtype)


def stacked(core, parts):
    rows, width = parts[0].shape
    cores = len(parts)
    out = jax.ShapeDtypeStruct((cores * rows, width), bf16)
    return one_step(
        functools.partial(stack_kernel, cores), core, list(parts), [None] * cores, [out], []
    )[0]


def sum_kernel(places, *refs):
    out = refs[-1]
    for row in range(0, out.shape[0], 128):
        total = jnp.zeros((128, out.shape[1]), f32)
        for ref, place in zip(refs[:-1], places):
            if place <= row < place + ref.shape[0]:
                total = total + ref[row - place : row - place + 128, :].astype(f32)
        out[row : row + 128, :] = total.astype(bf16)


def sum_of(wholes, shorter):
    parts = list(wholes) + [part for part, _ in shorter]
    places = [0] * len(wholes) + [place for _, place in shorter]
    return pl.pallas_call(
        functools.partial(sum_kernel, tuple(places)),
        out_shape=jax.ShapeDtypeStruct(wholes[0].shape, bf16),
        compiler_params=pltpu.CompilerParams(vmem_limit_bytes=60 << 20),
    )(*parts)


def product(left, right):
    return jnp.dot(left, right, preferred_element_type=f32)


def turn(value, distance):
    size = lax.axis_size("head")
    return lax.ppermute(value, "head", [(i, (i + distance) % size) for i in range(size)])


def others(value):
    return [turn(value, k) for k in range(1, lax.axis_size("head"))]


def in_order(parts, axis):
    size = len(parts)
    core = lax.axis_index("head")
    if size == 2:
        first, second = parts
        return jnp.where(
            core == 0,
            jnp.concatenate([first, second], axis=axis),
            jnp.concatenate([second, first], axis=axis),
        )
    ring = jnp.concatenate([parts[-k % size] for k in range(size)] * 2, axis=axis)
    length = parts[0].shape[axis]
    return lax.dynamic_slice_in_dim(ring, (size - core) % size * length, size * length, axis)


def shift(value, distance):
    devices = range(lax.axis_size("seq"))
    return lax.ppermute(value, "seq", [(i, i + distance) for i in devices if i + distance in devices])


def after(value, *first):
    return lax.optimization_barrier((value, first))[0]


class Ring:
    def __init__(self, size, step):
        self.size, self.step = size, step
        self.place = lax.axis_index("seq") // step % size

    def exchange(self, values):
        pairs = [[(i, i ^ k * self.step) for i in range(lax.axis_size("seq"))] for k in range(self.size)]
        return [lax.ppermute(values[k], "seq", pairs[k]) for k in range(1, self.size)]

    def cut(self, value, k):
        length = value.shape[0] // self.size
        return lax.dynamic_slice_in_dim(value, (self.place ^ k) * length, length, 0)

    def scatter(self, value):
        return self.exchange([self.cut(value, k) for k in range(self.size)])


def on_device(
    tokens,
    memory,
    cotangent,
    tgt_lengths,
    mem_lengths,
    self_query,
    self_key,
    self_value,
    self_output,
    cross_query,
    cross_key,
    cross_value,
    cross_output,
    hidden_in,
    hidden_out,
    prefix_keys,
    prefix_values,
    adapter_down,
    adapter_down_bias,
    adapter_up,
    adapter_up_bias,
):
    rows, width = tokens.shape
    cols = self_query.shape[1]
    prefix = prefix_keys.shape[0]
    shards = lax.axis_size("seq")
    position = lax.axis_index("seq")
    core = lax.axis_index("head")
    cores = lax.axis_size("head")
    total = rows * shards
    core_index = jnp.reshape(core, (1,)).astype(jnp.int32)

    def part_of(value, owner, axis=0):
        length = value.shape[axis] // cores
        return lax.dynamic_slice_in_dim(value, owner % cores * length, length, axis)

    def mine(value, axis=0):
        return part_of(value, core, axis)

    def dealt(parts):
        return [parts[0]] + [turn(parts[k], -k) for k in range(1, cores)]

    def over_cores(parts):
        arrived = [part.astype(f32) for part in dealt(parts)]
        return sum(arrived[1:], arrived[0])

    self_far = min(max(-(-(SEQ_MAX - rows) // 128) * 128, 0), rows)
    cross_far = min(max(-(-(SEQ_MAX + DRIFT - rows) // 128) * 128, 0), rows)
    self_base = rows + self_far
    far_rows = 2 * cross_far
    at = jnp.stack([position * rows, core]).astype(jnp.int32)
    base = 3 * rows + PAD
    far_spans = lambda at: (
        (at + rows + cross_far, at, at + cross_far),
        (at + cross_far - 2 * rows, at + cross_far, at + far_rows),
    )
    own_seen, halo_seen, main_seen, far_seen, here_seen, around_seen = see(
        (
            Span(((0, 0, rows),)),
            Span(((self_base, 0, self_base),)),
            Span(((rows, 0, 3 * rows),), False),
            Span(far_spans(0), False),
            Span(((0, 0, rows),), False),
            Span(((rows, 0, rows), (rows, 2 * rows, 3 * rows)) + far_spans(base), False),
        ),
        total,
        rows,
        tgt_lengths,
        mem_lengths,
        at,
    )

    tokens_cols = mine(tokens, 1)
    memory_cols = mine(after(memory, tokens_cols), 1)
    tokens_end = tokens_cols[rows - self_far :]
    token_near = shift(tokens_cols, 1)
    token_far = shift(tokens_end, 2)
    memory_after = shift(memory_cols, -1)
    down_biases = [adapter_down_bias] + others(adapter_down_bias)

    prefix_pad = ((0, 32 - prefix), (0, 0))
    prefix_rows = (
        jnp.pad(prefix_keys.astype(bf16), prefix_pad),
        jnp.pad(prefix_values.astype(bf16), prefix_pad),
        prefix,
    )

    query = (product(tokens, self_query) * (0.125 * LOG2E)).astype(bf16)

    own_keys = product(tokens, self_key).astype(bf16)
    own_values = product(tokens, self_value).astype(bf16)

    def all_cores(value, *first):
        return lax.all_gather(after(value, *first), "head", axis=0)

    self_outputs = all_cores(self_output, query)
    cross_queries = all_cores(cross_query, query)
    arrived = (token_near, token_far)
    memory_keys = product(memory, cross_key).astype(bf16)
    memory_values = product(memory, cross_value).astype(bf16)
    *state, own_keys, own_values = attend(
        query, [(own_keys, own_values)], (self_key, self_value), *own_seen, prefix_rows, last=False
    )
    arrived = (token_near, token_far, memory_after)
    ready = (state, memory_keys, memory_values)
    arrived, ready = lax.optimization_barrier((arrived, ready))
    token_near, token_far, memory_after = arrived
    state, memory_keys, memory_values = ready

    token_near = [token_near] + others(token_near)
    token_far = [token_far] + others(token_far)
    memory_after = [memory_after] + others(after(memory_after, token_near, token_far))
    memory_before = shift(after(memory_cols, token_near, token_far), 1)
    attended, self_lse, halo_keys, halo_values = attend(
        query,
        [Rows(token_far, self_far), Rows(token_near, rows)],
        (self_key, self_value),
        *halo_seen,
        state=state,
    )

    def to_rows(value):
        return [turn(part_of(value, core + k), k) for k in range(1, cores)]

    def to_heads(parts):
        parts = [parts[0]] + [turn(parts[k], -k) for k in range(1, cores)]
        return in_order([parts[-k % cores] for k in range(cores)], 0)

    cross_outputs = all_cores(cross_output, state)
    hidden_ins = all_cores(hidden_in, state)
    hidden_outs = all_cores(hidden_out, state)
    downs = all_cores(after(adapter_down, state).astype(bf16))
    ups = all_cores(after(adapter_up, state).astype(bf16))
    attended_rows = to_rows(attended)
    attended_rows, memory_before, memory_after = lax.optimization_barrier(
        (attended_rows, memory_before, memory_after)
    )
    memory_near = [[memory_before] + others(memory_before), memory_after]
    memory_far = (
        shift(after(memory_cols[rows - cross_far :], memory_near), 2),
        shift(after(memory_cols[:cross_far], memory_near), -2),
    )
    first, first_scale, cross_q = after_self(
        core_index, attended, attended_rows, self_outputs, cross_queries, tokens
    )

    cross_q = to_heads(cross_q)
    *state, main_keys, main_values = attend(
        cross_q,
        [Rows(memory_near[0], rows), (memory_keys, memory_values), Rows(memory_near[1], rows)],
        (cross_key, cross_value),
        *main_seen,
        last=False,
    )
    state, memory_far = lax.optimization_barrier((state, memory_far))
    memory_far = [Rows([part] + others(part), cross_far) for part in memory_far]
    crossed, cross_lse, far_keys, far_values = attend(
        cross_q, memory_far, (cross_key, cross_value), *far_seen, state=state
    )

    (
        outputs_rows,
        d_cross,
        d_crossed,
        adapter_grads,
    ) = feed_forward(
        core_index,
        crossed,
        to_rows(crossed),
        cross_outputs,
        first,
        cotangent,
        downs,
        down_biases,
        ups,
        adapter_up_bias,
        hidden_ins,
        hidden_outs,
    )
    d_crossed = to_heads(d_crossed)
    adapter_grads = dealt(after(adapter_grads, d_crossed))
    outputs_other = others(after(outputs_rows, d_crossed))
    ups_count = adapter_up.shape[0]
    staged = shards % 4 == 0 and shards & (shards - 1) == 0 and 2 * ups_count % shards == 0
    if staged:
        plane, column = Ring(4, 1), Ring(shards // 4, 4)

    adapter_grads, bias_grads = add_up([adapter_grads], 2 * ups_count)
    adapter_arrived = []
    if staged:
        adapter_kept = plane.cut(adapter_grads, 0)
        adapter_arrived = plane.scatter(adapter_grads)
        d_crossed = after(d_crossed, adapter_kept)

    cross_weights = (cross_key, cross_value)
    around_grads, query_state = attend_back(
        cross_q,
        d_crossed,
        crossed,
        [(main_keys, main_values, base), (far_keys, far_values, far_rows + PAD)],
        cross_weights,
        *around_seen,
        cross_lse,
        [(0, rows), (2 * rows, rows), (base, cross_far), (base + cross_far, cross_far)],
        cores,
    )
    around_grads, query_state, adapter_arrived, outputs_other = lax.optimization_barrier(
        (around_grads, query_state, adapter_arrived, outputs_other)
    )
    around_parts = [dealt(part) for part in around_grads]
    if staged:
        (adapter_grads,) = add_up([[adapter_kept] + adapter_arrived])
        around_parts = after(around_parts, adapter_grads)
    memory_low = add_up(around_parts)
    memory_arrived = [shift(memory_low[i], distance) for i, distance in enumerate((-1, 1, -2, 2))]
    adapter_arrived = []
    if staged:
        adapter_kept = column.cut(adapter_grads, 0)
        adapter_arrived = column.scatter(after(adapter_grads, memory_low))
        query_state = after(query_state, adapter_kept)
    query_state = after(query_state, memory_low)
    (memory_own,), cross_q_grad = attend_back(
        cross_q,
        d_crossed,
        crossed,
        [(memory_keys, memory_values, rows)],
        cross_weights,
        *here_seen,
        cross_lse,
        [(0, rows)],
        cores,
        state=query_state,
        final=True,
        pad=PAD,
    )
    cross_q_grad, memory_own, memory_near, adapter_arrived = lax.optimization_barrier(
        (cross_q_grad, memory_own, memory_arrived[:2], adapter_arrived)
    )
    grads_rows = to_rows(cross_q_grad)
    memory_own = dealt(after(memory_own, grads_rows))
    d_tokens, d_attended = before_self(
        core_index, cross_q_grad, grads_rows, cross_queries, self_outputs, d_cross, first,
        first_scale,
    )
    d_attended = to_heads(d_attended)
    d_tokens_cols = to_heads(d_tokens)
    memory_own, d_attended, d_tokens_cols = lax.optimization_barrier(
        (memory_own, d_attended, d_tokens_cols)
    )

    self_weights = (self_key, self_value, self_query)
    halo_grads, prefix_key_grad, prefix_value_grad, query_state = attend_back(
        query,
        d_attended,
        attended,
        [(halo_keys, halo_values, self_base + PAD)],
        self_weights,
        *halo_seen,
        self_lse,
        [(0, self_far), (self_far, rows)],
        cores,
        prefix_rows,
    )
    halo_grads, query_state, memory_far = lax.optimization_barrier(
        (halo_grads, query_state, memory_arrived[2:])
    )
    halo_parts = [dealt(part) for part in halo_grads]
    kept = [adapter_kept] + adapter_arrived if staged else [adapter_grads]
    both = pack(kept, prefix_key_grad, prefix_value_grad, bias_grads)
    halo_low = add_up(after(halo_parts, both))
    halo_arrived = (shift(halo_low[0], -2), shift(halo_low[1], -1))
    memory_own, memory_near, memory_far, outputs_rows, outputs_other = after(
        (memory_own, memory_near, memory_far, outputs_rows, outputs_other), halo_low
    )
    memory_sum = sum_of(
        memory_own + list(memory_near), [(memory_far[0], rows - cross_far), (memory_far[1], 0)]
    )
    grad_memory = beside(core_index, [memory_sum] + others(memory_sum))
    outputs = stacked(core_index, [outputs_rows] + outputs_other)
    query_state, grad_memory, outputs = lax.optimization_barrier((query_state, grad_memory, outputs))
    both_arrived = []
    if staged:
        both_arrived = column.exchange([after(both, grad_memory)] * column.size)
    ((here_grads,),) = attend_back(
        query,
        d_attended,
        attended,
        [(own_keys, own_values, rows + PAD)],
        self_weights,
        *own_seen,
        self_lse,
        [(0, rows)],
        cores,
        own=0,
        state=query_state,
    )
    here_grads, halo_arrived, both_arrived = lax.optimization_barrier(
        (here_grads, halo_arrived, both_arrived)
    )
    here_sum = over_cores(here_grads)
    if staged:
        place = jnp.reshape(column.place, (1,)).astype(jnp.int32)
        (both,) = gather_rows(place, [both] + both_arrived, None)
        parts = [both] + plane.exchange([both] * plane.size)
    token_sum = (
        d_tokens_cols.astype(f32)
        + here_sum
        + jnp.pad(halo_arrived[0], ((rows - self_far, 0), (0, 0))).astype(f32)
        + halo_arrived[1].astype(f32)
    ).astype(bf16)
    token_other = others(token_sum)
    grad_tokens = beside(core_index, [token_sum] + token_other)
    if staged:
        place = jnp.reshape(plane.place, (1,)).astype(jnp.int32)
    else:
        parts, place = [lax.psum(both, "seq")], core_index * 0
    parts = after(parts, grad_tokens)
    sizes = (prefix, cols, ups_count)
    prefix_k, prefix_v, grad_down, grad_down_bias, grad_up, grad_up_bias = gather_rows(place, parts, sizes)
    return (
        outputs,
        grad_tokens,
        grad_memory,
        prefix_k,
        prefix_v,
        grad_down,
        grad_down_bias[0],
        grad_up,
        grad_up_bias[0],
    )


def solution(mesh):
    in_specs = (
        P("seq", None),
        P("seq", None),
        P("seq", None),
        P(),
        P(),
        P(None, "head"),
        P(None, "head"),
        P(None, "head"),
        P("head", None),
        P(None, "head"),
        P(None, "head"),
        P(None, "head"),
        P("head", None),
        P(None, "head"),
        P("head", None),
        P(None, "head"),
        P(None, "head"),
        P(None, "head"),
        P("head"),
        P("head", None),
        P(),
    )
    out_specs = (
        P("seq", None),
        P("seq", None),
        P("seq", None),
        P(None, "head"),
        P(None, "head"),
        P(None, "head"),
        P("head"),
        P("head", None),
        P(),
    )
    return jax.shard_map(
        on_device, mesh=mesh, in_specs=in_specs, out_specs=out_specs, check_vma=False
    )
```

```python
import functools
from typing import NamedTuple

import jax
import jax.numpy as jnp
from jax import lax
from jax.experimental import pallas as pl
from jax.experimental.pallas import tpu as pltpu
from jax.sharding import PartitionSpec as P

HEAD_DIM = 64
MASKED = -1e30
LN2 = 0.6931471805599453
LOG2E = 1.4426950408889634
EPS = 1e-05
SEQ_MAX = 1792
DRIFT = 128
PAD = 128
BLOCK = 256
f32 = jnp.float32
bf16 = jnp.bfloat16


def dot(left, right):
    return jnp.dot(left, right, preferred_element_type=f32)


def dot_nt(left, right):
    return lax.dot_general(left, right, (((1,), (1,)), ((), ())), preferred_element_type=f32)


def dot_tn(left, right):
    return lax.dot_general(left, right, (((0,), (0,)), ((), ())), preferred_element_type=f32)


def split_rows(pair):
    zero = jnp.zeros((HEAD_DIM, pair.shape[1]), pair.dtype)
    return [
        jnp.concatenate([pair[:HEAD_DIM], zero], axis=0),
        jnp.concatenate([zero, pair[HEAD_DIM:]], axis=0),
    ]


def stack_lanes(pair):
    first = lax.broadcasted_iota(jnp.int32, pair.shape, 1) < HEAD_DIM
    zero = jnp.zeros_like(pair)
    return jnp.concatenate([jnp.where(first, pair, zero), jnp.where(first, zero, pair)], axis=0)


def over_range(low, high, body):
    def step(i, carry):
        body(pl.ds(pl.multiple_of(low + i * 128, 128), 128))
        return carry

    lax.fori_loop(0, pl.cdiv(high - low, 128), step, 0)


def over_tiles(info, segments, block, tile):
    def one_segment(segment, carry):
        first, count, low, high = (info[6 * segment + i, block] for i in range(4))

        def full(i, carry):
            tile(pl.multiple_of(first + i * BLOCK, 128), segment, False)
            return carry

        def edge(j, carry):
            i = jnp.where(j < low, j, j - low + high)
            tile(pl.multiple_of(first + i * BLOCK, 128), segment, True)
            return carry

        lax.fori_loop(low, high, full, 0)
        lax.fori_loop(0, low + count - high, edge, 0)
        return carry

    if segments == 1:
        one_segment(0, 0)
    else:
        lax.fori_loop(0, segments, one_segment, 0)


def span_of(info, segment):
    return info[6 * segment + 4, 0], info[6 * segment + 5, 0]


def in_spans(info, segments, test):
    result = test(*span_of(info, 0))
    for segment in range(1, segments):
        result = result | test(*span_of(info, segment))
    return result


def owned(info, segments, cores, before, length):
    owner = lax.rem(info[6 * segments, 0] + cores - before, cores)
    return pl.ds(pl.multiple_of(owner * length, length), length)


def allowed(row, start, end):
    place = row + lax.broadcasted_iota(jnp.int32, (BLOCK, start.shape[1]), 0)
    return (place >= start) & (place < end)


def pair_cols(head):
    return slice(head // 2 * 128, head // 2 * 128 + 128)


def head_rows(head):
    return slice(head * HEAD_DIM, head * HEAD_DIM + HEAD_DIM)


def attend_kernel(prefix, resume, last, segments, pieces, cores, info, *refs):
    refs = list(refs)
    q, start, end = refs[:3]
    del refs[:3]
    wk, wv = refs[:2]
    del refs[:2]
    parts = []
    for length, raw in pieces:
        count = cores if raw else 2
        parts.append(refs[:count])
        del refs[:count]
    if prefix:
        pk, pv = refs[:2]
        del refs[:2]
    if resume:
        top_in, total_in, acc_in = refs[:3]
        del refs[:3]
    outs = refs[: 2 if last else 3]
    del refs[: len(outs)]
    k, v = refs[:2]
    del refs[:2]
    vt = refs.pop(0)
    if last:
        out, lse = outs
        top, total, acc = refs[:3]
        del refs[:3]
    else:
        top, total, acc = outs
    block = pl.program_id(0)
    heads = q.shape[1] // HEAD_DIM

    def bring(piece, offset, length, sem):
        window = pl.ds(offset, length)
        return (
            pltpu.make_async_copy(piece[0], k.at[window, :], sem.at[0]),
            pltpu.make_async_copy(piece[1], v.at[window, :], sem.at[1]),
        )

    def project(piece, offset, length):
        def rows_at(row, size):
            window = pl.ds(offset + row, size)

            needed = lambda least, most: (offset + row < most) & (offset + row + size > least)

            @pl.when(in_spans(info, segments, needed))
            def _():
                source = pl.ds(row, size)
                depth = piece[0].shape[1]
                new_k, new_v = 0.0, 0.0
                for core, part in enumerate(piece):
                    some = owned(info, segments, cores, core, depth)
                    value = part[source, :]
                    new_k = new_k + dot(value, wk[some, :])
                    new_v = new_v + dot(value, wv[some, :])
                k[window, :] = new_k.astype(bf16)
                new_v = new_v.astype(bf16)
                v[window, :] = new_v
                vt[:, window] = new_v.T

        def step(i, carry):
            rows_at(pl.multiple_of(i * BLOCK, BLOCK), BLOCK)
            return carry

        full = length // BLOCK
        lax.fori_loop(0, full, step, 0)
        if length % BLOCK:
            rows_at(full * BLOCK, length % BLOCK)

    def turn_over(window):
        vt[:, window] = v[window, :].T

    @pl.when(block == 0)
    def _():
        offset, ready = 0, []
        for (length, raw), piece in zip(pieces, parts):
            if not raw:
                for copy in bring(piece, offset, length, refs[0]):
                    copy.start()
            offset += length
        rest = slice(offset, k.shape[0])
        k[rest, :] = jnp.zeros((k.shape[0] - offset, k.shape[1]), bf16)
        v[rest, :] = jnp.zeros((k.shape[0] - offset, k.shape[1]), bf16)
        vt[:, rest] = jnp.zeros((k.shape[1], k.shape[0] - offset), bf16)
        offset = 0
        for (length, raw), piece in zip(pieces, parts):
            if raw:
                project(piece, offset, length)
            offset += length
        offset = 0
        for (length, raw), piece in zip(pieces, parts):
            if not raw:
                for copy in bring(piece, offset, length, refs[0]):
                    copy.wait()
                for segment in range(segments):
                    least, most = span_of(info, segment)
                    over_range(
                        jnp.maximum(least, offset), jnp.minimum(most, offset + length), turn_over
                    )
            offset += length

    qs = []
    for pair in range(heads // 2):
        qs.extend(split_rows(q[:, pair * 128 : pair * 128 + 128].T))
    if resume:
        top[...] = top_in[...]
        total[...] = total_in[...]
        acc[...] = acc_in[...]
    elif prefix:
        there = lax.broadcasted_iota(jnp.int32, (32, BLOCK), 0) < prefix
        for head in range(heads):
            scores = jnp.where(there, dot(pk[:, pair_cols(head)], qs[head]), MASKED)
            peak = jnp.max(scores, axis=0, keepdims=True)
            weights = jnp.exp2(scores - peak)
            top[head : head + 1] = peak
            total[head : head + 1] = jnp.sum(weights, axis=0, keepdims=True)
            turned = pv[:, pair_cols(head)].T
            acc[head_rows(head)] = dot(turned[head_rows(head % 2)], weights.astype(bf16))
    else:
        top[...] = jnp.full(top.shape, MASKED, f32)
        total[...] = jnp.zeros(total.shape, f32)
        acc[...] = jnp.zeros(acc.shape, f32)

    def tile(row, segment, edge):
        window = pl.ds(row, BLOCK)
        if edge:
            seen = pl.ds(segment, 1)
            open_ = allowed(row, start[seen, :], end[seen, :])
        scores = [dot(k[window, pair_cols(head)], qs[head]) for head in range(heads)]
        for head in range(heads):
            score = scores[head]
            if edge:
                score = jnp.where(open_, score, MASKED)
            old = top[head : head + 1]
            peak = jnp.maximum(old, jnp.max(score, axis=0, keepdims=True))
            weights = jnp.exp2(score - peak)
            scale = jnp.exp2(old - peak)
            top[head : head + 1] = peak
            total[head : head + 1] = total[head : head + 1] * scale + jnp.sum(
                weights, axis=0, keepdims=True
            )
            acc[head_rows(head)] = acc[head_rows(head)] * scale + dot(
                vt[head_rows(head), window], weights.astype(bf16)
            )

    over_tiles(info, segments, block, tile)
    if last:
        for pair in range(heads // 2):
            parts = [
                acc[head_rows(head)] * (1.0 / total[head : head + 1])
                for head in (2 * pair, 2 * pair + 1)
            ]
            out[:, pair * 128 : pair * 128 + 128] = (
                jnp.concatenate(parts, axis=0).T.astype(bf16)
            )
        lse[...] = top[...] + jnp.log2(total[...])


def kernel_params():
    return pltpu.CompilerParams(
        dimension_semantics=("arbitrary",), vmem_limit_bytes=60 << 20
    )


class Rows(NamedTuple):
    parts: list
    length: int


def attend(query, keys, weights, start, end, info, prefix=None, state=None, last=True):
    rows, cols = query.shape
    heads = cols // HEAD_DIM
    by_rows = pl.BlockSpec((BLOCK, cols), lambda b, info: (b, 0))
    by_lanes = lambda count: pl.BlockSpec((count, BLOCK), lambda b, info: (0, b))
    whole = lambda count, wide=cols: pl.BlockSpec((count, wide), lambda b, info: (0, 0))
    segments = start.shape[0]
    operands = [query, start, end]
    specs = [by_rows, by_lanes(segments), by_lanes(segments)]
    cores = 1
    pieces = tuple(
        (piece.length, True) if isinstance(piece, Rows) else (piece[0].shape[0], False)
        for piece in keys
    )
    window = sum(length for length, raw in pieces) + PAD
    operands += list(weights)
    specs += [whole(weights[0].shape[0])] * 2
    for (length, raw), piece in zip(pieces, keys):
        if raw:
            cores = len(piece.parts)
            operands += list(piece.parts)
            specs += [whole(length, part.shape[1]) for part in piece.parts]
        else:
            operands += list(piece)
            specs += [pl.BlockSpec(memory_space=pl.ANY)] * 2
    if prefix is not None:
        operands += [prefix[0], prefix[1]]
        specs += [whole(32), whole(32)]
    state_specs = [by_lanes(heads), by_lanes(heads), by_lanes(cols)]
    if state is not None:
        operands += list(state)
        specs += state_specs
    shape = jax.ShapeDtypeStruct
    scratch = [pltpu.VMEM((cols, window), bf16)]
    if last:
        outs = [shape((rows, cols), bf16), shape((heads, rows), f32)]
        out_specs = [by_rows, by_lanes(heads)]
        scratch += [pltpu.VMEM((n, BLOCK), f32) for n in (heads, heads, cols)]
    else:
        outs = [shape((n, rows), f32) for n in (heads, heads, cols)]
        out_specs = list(state_specs)
    outs += [shape((window, cols), bf16)] * 2
    out_specs += [whole(window)] * 2
    scratch.append(pltpu.SemaphoreType.DMA((2,)))
    return pl.pallas_call(
        functools.partial(
            attend_kernel, 0 if prefix is None else prefix[2], state is not None, last, segments,
            pieces, cores,
        ),
        out_shape=tuple(outs),
        grid_spec=pltpu.PrefetchScalarGridSpec(
            num_scalar_prefetch=1,
            grid=(rows // BLOCK,),
            in_specs=specs,
            out_specs=tuple(out_specs),
            scratch_shapes=scratch,
        ),
        compiler_params=kernel_params(),
    )(info, *operands)


def attend_back_kernel(
    prefix, resume, own, final, lengths, cuts, cores, segments, info, *refs
):
    refs = list(refs)
    q, d_out, out, start, end, lse, wk, wv = refs[:8]
    del refs[:8]
    sources = [refs[2 * i : 2 * i + 2] for i in range(len(lengths))]
    del refs[: 2 * len(lengths)]
    if prefix:
        pk, pv = refs[:2]
        del refs[:2]
    if resume:
        dq_in = refs.pop(0)
    if own is not None:
        wq = refs.pop(0)
    pieces = len(cuts)
    grads = [refs[i * cores : i * cores + cores] for i in range(pieces)]
    del refs[: pieces * cores]
    if prefix:
        dpk, dpv = refs[:2]
        del refs[:2]
    if own is None:
        dq_out = refs.pop(0)
    k, v, kt, dk, dv, dq, sem = refs[:7]
    if own is not None:
        dq_low = refs[7]
    block = pl.program_id(0)
    heads = q.shape[1] // HEAD_DIM
    pairs = heads // 2

    @pl.when(block == 0)
    def _():
        copies, offset = [], 0
        for i, (length, source) in enumerate(zip(lengths, sources)):
            for j, (there, here) in enumerate(zip(source, (k, v))):
                copies.append(
                    pltpu.make_async_copy(
                        there.at[pl.ds(0, length), :],
                        here.at[pl.ds(offset, length), :],
                        sem.at[2 * i + j],
                    )
                )
            offset += length
        for copy in copies:
            copy.start()
        if offset < k.shape[0]:
            rest = slice(offset, k.shape[0])
            k[rest, :] = jnp.zeros((k.shape[0] - offset, k.shape[1]), bf16)
            v[rest, :] = jnp.zeros((k.shape[0] - offset, k.shape[1]), bf16)
        if prefix:
            dpk[...] = jnp.zeros(dpk.shape, f32)
            dpv[...] = jnp.zeros(dpv.shape, f32)

        def clear(window):
            dk[window, :] = jnp.zeros((128, dk.shape[1]), f32)
            dv[window, :] = jnp.zeros((128, dv.shape[1]), f32)

        def turn_over(window):
            kt[:, window] = k[window, :].T

        for segment in range(segments):
            over_range(*span_of(info, segment), clear)
        for copy in copies:
            copy.wait()
        for segment in range(segments):
            over_range(*span_of(info, segment), turn_over)

    qs, ds, delta, q_stack, d_stack = [], [], [], [], []
    for pair in range(pairs):
        cols = slice(pair * 128, pair * 128 + 128)
        q_pair, d_pair = q[:, cols], d_out[:, cols]
        qs.extend(split_rows(q_pair.T))
        ds.extend(split_rows(d_pair.T))
        both = (d_pair.astype(f32) * out[:, cols].astype(f32)).T
        delta.append(jnp.sum(both[:HEAD_DIM], axis=0, keepdims=True))
        delta.append(jnp.sum(both[HEAD_DIM:], axis=0, keepdims=True))
        q_stack.append(stack_lanes(q_pair))
        d_stack.append(stack_lanes(d_pair))
    if resume:
        dq[...] = dq_in[...]
    else:
        dq[...] = jnp.zeros(dq.shape, f32)
    if prefix:
        there = lax.broadcasted_iota(jnp.int32, (32, BLOCK), 0) < prefix
        for pair in range(pairs):
            cols = slice(pair * 128, pair * 128 + 128)
            turned = pk[:, cols].T
            ws, gs = [], []
            for head in (2 * pair, 2 * pair + 1):
                scores = dot(pk[:, cols], qs[head])
                weights = jnp.where(there, jnp.exp2(scores - lse[head : head + 1]), 0.0)
                grad = (weights * (dot(pv[:, cols], ds[head]) - delta[head])).astype(bf16)
                dq[head_rows(head)] += dot(turned[head_rows(head % 2)], grad)
                ws.append(weights.astype(bf16))
                gs.append(grad)
            dpv[:, cols] += dot(jnp.concatenate(ws, axis=1), d_stack[pair])
            dpk[:, cols] += dot(jnp.concatenate(gs, axis=1), q_stack[pair]) * LN2

    def tile(row, segment, edge):
        window = pl.ds(row, BLOCK)
        if edge:
            seen = pl.ds(segment, 1)
            open_ = allowed(row, start[seen, :], end[seen, :])
        scores = [dot(k[window, pair_cols(head)], qs[head]) for head in range(heads)]
        inner = [dot(v[window, pair_cols(head)], ds[head]) for head in range(heads)]
        for pair in range(pairs):
            cols = slice(pair * 128, pair * 128 + 128)
            ws, gs = [], []
            for head in (2 * pair, 2 * pair + 1):
                weights = jnp.exp2(scores[head] - lse[head : head + 1])
                if edge:
                    weights = jnp.where(open_, weights, 0.0)
                grad = (weights * (inner[head] - delta[head])).astype(bf16)
                dq[head_rows(head)] += dot(kt[head_rows(head), window], grad)
                ws.append(weights.astype(bf16))
                gs.append(grad)
            dv[window, cols] += dot(jnp.concatenate(ws, axis=1), d_stack[pair])
            dk[window, cols] += dot(jnp.concatenate(gs, axis=1), q_stack[pair])

    over_tiles(info, segments, block, tile)
    if own is None and final:
        dq_out[...] = (dq[...] * 0.125).T.astype(bf16)
    elif own is None:
        dq_out[...] = dq[...]
    else:
        dq_low[pl.ds(pl.multiple_of(block * BLOCK, BLOCK), BLOCK), :] = (
            (dq[...] * 0.125).T.astype(bf16)
        )

    @pl.when(block == pl.num_programs(0) - 1)
    def _():
        def project(row, size, piece, offset):
            window = pl.ds(row, size)
            target = pl.ds(offset, size)
            touched = in_spans(
                info, segments, lambda least, most: (row < most) & (row + size > least)
            )
            width = grads[piece][0].shape[1]

            @pl.when(touched)
            def _():
                place = row + lax.broadcasted_iota(jnp.int32, (size, dk.shape[1]), 0)
                there = in_spans(
                    info, segments, lambda least, most: (place >= least) & (place < most)
                )
                dk_low = jnp.where(there, dk[window, :] * LN2, 0.0).astype(bf16)
                dv_low = jnp.where(there, dv[window, :], 0.0).astype(bf16)
                for core in range(cores):
                    part = owned(info, segments, cores, core, width)
                    value = dot_nt(dk_low, wk[part, :]) + dot_nt(dv_low, wv[part, :])
                    if own == piece:
                        value += dot_nt(dq_low[target, :], wq[part, :])
                    grads[piece][core][target, :] = value.astype(bf16)

            @pl.when(jnp.logical_not(touched))
            def _():
                for core in range(cores):
                    value = jnp.zeros((size, width), f32)
                    if own == piece:
                        part = owned(info, segments, cores, core, width)
                        value = dot_nt(dq_low[target, :], wq[part, :])
                    grads[piece][core][target, :] = value.astype(bf16)

        for piece, (begin, length) in enumerate(cuts):
            whole = length // BLOCK

            def step(i, carry, piece=piece, begin=begin):
                offset = pl.multiple_of(i * BLOCK, BLOCK)
                project(pl.multiple_of(begin + offset, 128), BLOCK, piece, offset)
                return carry

            lax.fori_loop(0, whole, step, 0)
            rest = length - whole * BLOCK
            if rest:
                project(begin + whole * BLOCK, rest, piece, whole * BLOCK)


def attend_back(
    query, d_out, out, sources, weights, start, end, info, lse, cuts, cores, prefix=None, own=None,
    state=None, final=False, pad=0,
):
    rows, cols = query.shape
    lengths = tuple(length for _, _, length in sources)
    window = sum(lengths) + pad
    width = weights[0].shape[0]
    heads = cols // HEAD_DIM
    segments = start.shape[0]
    by_rows = pl.BlockSpec((BLOCK, cols), lambda b, info: (b, 0))
    by_lanes = lambda count: pl.BlockSpec((count, BLOCK), lambda b, info: (0, b))
    whole = lambda count, wide=cols: pl.BlockSpec((count, wide), lambda b, info: (0, 0))
    operands = [query, d_out, out, start, end, lse] + list(weights[:2])
    specs = [by_rows] * 3 + [by_lanes(segments)] * 2 + [by_lanes(heads)] + [whole(width)] * 2
    for keys, values, _ in sources:
        operands += [keys, values]
        specs += [pl.BlockSpec(memory_space=pl.ANY)] * 2
    if prefix is not None:
        operands += [prefix[0], prefix[1]]
        specs += [whole(32), whole(32)]
    if state is not None:
        operands.append(state)
        specs.append(by_lanes(cols))
    if own is not None:
        operands.append(weights[2])
        specs.append(whole(width))
    shape = jax.ShapeDtypeStruct
    outs, out_specs = [], []
    for _, length in cuts:
        outs += [shape((length, width // cores), bf16)] * cores
        out_specs += [whole(length, width // cores)] * cores
    if prefix is not None:
        outs += [shape((32, cols), f32)] * 2
        out_specs += [whole(32)] * 2
    if own is None and final:
        outs.append(shape((rows, cols), bf16))
        out_specs.append(by_rows)
    elif own is None:
        outs.append(shape((cols, rows), f32))
        out_specs.append(by_lanes(cols))
    scratch = [
        pltpu.VMEM((window, cols), bf16),
        pltpu.VMEM((window, cols), bf16),
        pltpu.VMEM((cols, window), bf16),
        pltpu.VMEM((window, cols), f32),
        pltpu.VMEM((window, cols), f32),
        pltpu.VMEM((cols, BLOCK), f32),
        pltpu.SemaphoreType.DMA((2 * len(sources),)),
    ]
    if own is not None:
        scratch.append(pltpu.VMEM((rows, cols), bf16))
    result = pl.pallas_call(
        functools.partial(
            attend_back_kernel, 0 if prefix is None else prefix[2], state is not None, own, final,
            lengths, tuple(cuts), cores, segments,
        ),
        out_shape=tuple(outs),
        grid_spec=pltpu.PrefetchScalarGridSpec(
            num_scalar_prefetch=1,
            grid=(rows // BLOCK,),
            in_specs=specs,
            out_specs=tuple(out_specs),
            scratch_shapes=scratch,
        ),
        compiler_params=kernel_params(),
    )(info, *operands)
    pieces = [list(result[i * cores : i * cores + cores]) for i in range(len(cuts))]
    return pieces, *result[len(cuts) * cores :]


class Span(NamedTuple):
    segments: tuple
    causal: bool = True


def spans_kernel(spans, total, rows, tgt, mem, at, *refs):
    here, core = at[0], at[1]
    place = here + lax.broadcasted_iota(jnp.int32, (1, rows), 1)

    def one(j, carry):
        begin, mem_begin, start, mem_start, mem_end = carry
        end, mem_stop = begin + tgt[j], mem_begin + mem[j]
        past = place >= end
        start = jnp.where(past, end, start)
        mem_start = jnp.where(past, mem_stop, mem_start)
        mem_end = jnp.where(place >= begin, mem_stop, mem_end)
        return end, mem_stop, start, mem_start, mem_end

    zero = jnp.zeros((1, rows), jnp.int32)
    begin, _, start, mem_start, mem_end = lax.fori_loop(
        0, tgt.shape[0], one, (0, 0, zero, zero, zero)
    )
    mem_end = jnp.where(place >= begin, total, mem_end)
    blocks = rows // BLOCK

    def least(value, block):
        part = value[:, block * BLOCK : block * BLOCK + BLOCK].astype(f32)
        return jnp.min(part).astype(jnp.int32)

    def most(value, block):
        part = value[:, block * BLOCK : block * BLOCK + BLOCK].astype(f32)
        return jnp.max(part).astype(jnp.int32)

    ends = [
        [(least(value, b), most(value, b)) for b in range(blocks)]
        for value in (start - here, mem_start - here, mem_end - here)
    ]
    for i, span in enumerate(spans):
        starts_out, ends_out, info = refs[3 * i : 3 * i + 3]
        for segment, (base, low, high) in enumerate(span.segments):
            clip = lambda value: jnp.clip(value + base, low, high)
            if span.causal:
                lows, highs = start - here, place - here + 1
                corners = [(ends[0][b], (b * BLOCK + 1, b * BLOCK + BLOCK)) for b in range(blocks)]
            else:
                lows, highs = mem_start - here, mem_end - here
                corners = [(ends[1][b], ends[2][b]) for b in range(blocks)]
            starts_out[segment : segment + 1, :] = clip(lows)
            ends_out[segment : segment + 1, :] = clip(highs)
            lowest, highest = 1 << 20, 0
            for b, ((s0, s1), (e0, e1)) in enumerate(corners):
                s0, s1, e0, e1 = clip(s0), clip(s1), clip(e0), clip(e1)
                some = e1 > s0
                first = jnp.where(some, s0 // 128 * 128, 0)
                count = jnp.where(some, (e1 - first + BLOCK - 1) // BLOCK, 0)
                from_ = jnp.clip((s1 - first + BLOCK - 1) // BLOCK, 0, count)
                to = jnp.clip((e0 - first) // BLOCK, from_, count)
                for row, value in enumerate((first, count, from_, to)):
                    info[6 * segment + row, b] = value
                lowest = jnp.where(some, jnp.minimum(lowest, first), lowest)
                highest = jnp.where(some, jnp.maximum(highest, first + count * BLOCK), highest)
            for b in range(blocks):
                info[6 * segment + 4, b] = jnp.minimum(lowest, highest)
                info[6 * segment + 5, b] = highest
        for b in range(blocks):
            info[6 * len(span.segments), b] = core


def see(spans, total, rows, tgt, mem, at):
    outs, specs = [], []
    for span in spans:
        count = len(span.segments)
        outs += [jax.ShapeDtypeStruct((count, rows), jnp.int32)] * 2
        outs.append(jax.ShapeDtypeStruct((6 * count + 1, rows // BLOCK), jnp.int32))
        specs += [pl.BlockSpec((count, rows), lambda i, *scalars: (0, 0))] * 2
        specs.append(pl.BlockSpec(memory_space=pltpu.SMEM))
    result = pl.pallas_call(
        functools.partial(spans_kernel, spans, total, rows),
        out_shape=tuple(outs),
        grid_spec=pltpu.PrefetchScalarGridSpec(
            num_scalar_prefetch=3, grid=(1,), in_specs=[], out_specs=tuple(specs)
        ),
    )(tgt, mem, at)
    return [result[3 * i : 3 * i + 3] for i in range(len(spans))]


def norm_parts(value):
    center = value - jnp.mean(value, axis=-1, keepdims=True)
    scale = lax.rsqrt(jnp.mean(center * center, axis=-1, keepdims=True) + EPS)
    return center * scale, scale


def norm_back(normal, scale, grad):
    return scale * (
        grad
        - jnp.mean(grad, axis=-1, keepdims=True)
        - normal * jnp.mean(grad * normal, axis=-1, keepdims=True)
    )


def gelu_pair(value):
    size = jnp.abs(value)
    bell = jnp.exp(-0.5 * value * value)
    under = 1.0 + (0.3275911 * 0.7071067811865476) * size
    t = pl.reciprocal(under, approx=True)
    t = t * (2.0 - under * t)
    poly = ((((1.061405429 * t - 1.453152027) * t + 1.421413741) * t - 0.284496736) * t + 0.254829592) * t
    tail = 0.5 * poly * bell
    cdf = jnp.where(value >= 0, 1.0 - tail, tail)
    return value * cdf, cdf + value * (0.3989422804014327 * bell)


def ffn_kernel(cores, chunk, core, *refs):
    refs = list(refs)

    def take(count):
        taken = refs[:count]
        del refs[:count]
        return taken

    crossed = take(cores)
    cross_outs = take(cores)
    first, cot = take(2)
    downs = take(cores)
    biases = take(cores)
    ups = take(cores)
    (up_bias,) = take(1)
    hins, houts = take(2)
    cross_outs, downs, ups = ([ref.at[0] for ref in part] for part in (cross_outs, downs, ups))
    out, d_cross = take(2)
    d_crossed = take(cores)
    adapter_grads = take(cores)
    hin, hout, in_sem, out_sem, slope, bufs0, bufs1, branch, second, second_low, adapted, down_slope, low = refs
    per = hins.shape[2] // chunk
    count = per * cores
    adapt = downs[0].shape[1]

    def copies(j):
        c, i = divmod(j, per)
        part = pl.ds(i * chunk, chunk)
        return (
            pltpu.make_async_copy(hins.at[c, :, part], hin.at[j], in_sem.at[j]),
            pltpu.make_async_copy(houts.at[c, part, :], hout.at[j], out_sem.at[j]),
        )

    for j in range(count):
        for copy in copies(j):
            copy.start()
    total = first[...]
    for value, weight in zip(crossed, cross_outs):
        total = total + dot(value[...], weight[...])
    normal, scale2 = norm_parts(total)
    second[...] = normal
    second_low[...] = normal.astype(bf16)

    wide = 4.0 * up_bias[...]
    acc = jnp.zeros(branch.shape, f32)
    for c in range(cores):
        part = slice(c * adapt, (c + 1) * adapt)
        value, grad = gelu_pair(dot(second_low[...], downs[c][...]) + biases[c][...])
        adapted[:, part] = value.astype(bf16)
        down_slope[:, part] = grad
        acc = acc + dot(adapted[:, part], ups[c][...])
    branch[...] = 4.0 * acc + wide

    for j in range(count):
        for copy in copies(j):
            copy.wait()
    bufs0[...] = dot(second_low[...], hin[0])

    def forward(j, now, later):
        later[...] = dot(second_low[...], hin[jnp.minimum(j + 1, count - 1)])
        value, grad = gelu_pair(now[...])
        slope[j] = grad.astype(bf16)
        branch[...] += dot(value.astype(bf16), hout[j])

    def forward_two(i, _):
        forward(2 * i, bufs0, bufs1)
        forward(2 * i + 1, bufs1, bufs0)
        return 0

    lax.fori_loop(0, count // 2, forward_two, 0)
    normal, scale = norm_parts(second[...] + branch[...])
    out[...] = normal.astype(bf16)
    d_third = norm_back(normal, scale, cot[...].astype(f32))
    branch[...] = d_third
    low[...] = d_third.astype(bf16)
    up_sum = 4.0 * jnp.sum(low[...].astype(f32), axis=0, keepdims=True)
    line = lax.broadcasted_iota(jnp.int32, (16, up_sum.shape[1]), 0)

    def backward(j):
        value = (slope[j].astype(f32) * dot_nt(low[...], hout[j])).astype(bf16)
        branch[...] += dot_nt(value, hin[j])

    def backward_two(i, _):
        backward(2 * i)
        backward(2 * i + 1)
        return 0

    lax.fori_loop(0, count // 2, backward_two, 0)
    total = branch[...]
    for c in range(cores):
        part = slice(c * adapt, (c + 1) * adapt)
        value = (down_slope[:, part] * (4.0 * dot_nt(low[...], ups[c][...]))).astype(bf16)
        total = total + dot_nt(value, downs[c][...])
        adapter_grads[c][adapt : 2 * adapt, :] = dot_tn(value, second_low[...]).astype(bf16)
        adapter_grads[c][:adapt, :] = (4.0 * dot_tn(adapted[:, part], low[...])).astype(bf16)
        down_sum = jnp.sum(value.astype(f32), axis=0, keepdims=True)
        down_sum = jnp.concatenate(
            [down_sum, jnp.zeros((1, up_sum.shape[1] - adapt), f32)], axis=1
        )
        biases_low = jnp.where(line == 0, up_sum, jnp.where(line == 1, down_sum, 0.0))
        adapter_grads[c][2 * adapt :, :] = biases_low.astype(bf16)
    d_second = norm_back(second[...], scale2, total)
    d_cross[...] = d_second
    for result, weight in zip(d_crossed, cross_outs):
        result[...] = dot_nt(d_second.astype(bf16), weight[...]).astype(bf16)


def at_core(cores, rows, width):
    return pl.BlockSpec((rows, width), lambda i, core: (core[0], 0))


def down_from_core(cores, shape):
    def spec(k):
        return pl.BlockSpec(
            (1,) + shape, lambda i, core: (lax.rem(core[0] + cores - k, cores), 0, 0)
        )

    return [spec(k) for k in range(cores)]


def one_step(kernel, core, operands, specs, outs, scratch):
    whole = lambda shape: pl.BlockSpec(shape, lambda i, core: (0,) * len(shape))
    specs = [whole(op.shape) if spec is None else spec for op, spec in zip(operands, specs)]
    return pl.pallas_call(
        kernel,
        out_shape=tuple(outs),
        grid_spec=pltpu.PrefetchScalarGridSpec(
            num_scalar_prefetch=1,
            grid=(1,),
            in_specs=specs,
            out_specs=tuple(whole(out.shape) for out in outs),
            scratch_shapes=scratch,
        ),
        compiler_params=kernel_params(),
    )(core, *operands)


def feed_forward(core, crossed, crossed_others, cross_outs, first, cot, downs, biases, ups, up_bias, hins, houts):
    rows, width = first.shape
    cores, _, hidden = hins.shape
    adapt = downs.shape[2]
    heads = crossed.shape[1]
    chunk = min(512, hidden)
    count = cores * hidden // chunk
    hbm = pl.BlockSpec(memory_space=pl.ANY)
    operands = [crossed] + list(crossed_others)
    specs = [at_core(cores, rows, heads)] + [None] * (cores - 1)
    operands += [cross_outs] * cores + [first, cot]
    specs += down_from_core(cores, cross_outs.shape[1:]) + [None, at_core(cores, rows, width)]
    operands += [downs] * cores + [bias[None] for bias in biases] + [ups] * cores + [up_bias[None]]
    specs += down_from_core(cores, downs.shape[1:]) + [None] * cores
    specs += down_from_core(cores, ups.shape[1:]) + [None]
    operands += [hins, houts]
    specs += [hbm, hbm]
    shape = jax.ShapeDtypeStruct
    outs = (
        [shape((rows, width), bf16), shape((rows, width), f32)]
        + [shape((rows, heads), bf16)] * cores
        + [shape((2 * adapt + 16, width), bf16)] * cores
    )
    scratch = [
        pltpu.VMEM((count, width, chunk), bf16),
        pltpu.VMEM((count, chunk, width), bf16),
        pltpu.SemaphoreType.DMA((count,)),
        pltpu.SemaphoreType.DMA((count,)),
        pltpu.VMEM((count, rows, chunk), bf16),
        pltpu.VMEM((rows, chunk), f32),
        pltpu.VMEM((rows, chunk), f32),
        pltpu.VMEM((rows, width), f32),
        pltpu.VMEM((rows, width), f32),
        pltpu.VMEM((rows, width), bf16),
        pltpu.VMEM((rows, adapt * cores), bf16),
        pltpu.VMEM((rows, adapt * cores), f32),
        pltpu.VMEM((rows, width), bf16),
    ]
    result = one_step(
        functools.partial(ffn_kernel, cores, chunk), core, operands, specs, outs, scratch
    )
    at = 2 + cores
    return result[0], result[1], list(result[2:at]), list(result[at:])


def after_self_kernel(cores, core, *refs):
    refs = list(refs)
    attended, refs = refs[:cores], refs[cores:]
    outputs, refs = refs[:cores], refs[cores:]
    queries, refs = refs[:cores], refs[cores:]
    tokens, first, scale = refs[:3]
    total = tokens[...].astype(f32)
    for value, weight in zip(attended, outputs):
        total = total + dot(value[...], weight[0])
    normal, inverse = norm_parts(total)
    first[...] = normal
    scale[...] = inverse
    low = normal.astype(bf16)
    for result, weight in zip(refs[3:], queries):
        result[...] = (dot(low, weight[0]) * (0.125 * LOG2E)).astype(bf16)


def after_self(core, attended, attended_others, outputs, queries, tokens):
    cores, heads, width = outputs.shape
    rows = tokens.shape[0] // cores
    operands = [attended] + list(attended_others) + [outputs] * cores + [queries] * cores + [tokens]
    specs = [at_core(cores, rows, heads)] + [None] * (cores - 1)
    specs += down_from_core(cores, outputs.shape[1:]) + down_from_core(cores, queries.shape[1:])
    specs += [at_core(cores, rows, width)]
    shape = jax.ShapeDtypeStruct
    outs = [shape((rows, width), f32), shape((rows, 1), f32)] + [shape((rows, heads), bf16)] * cores
    result = one_step(
        functools.partial(after_self_kernel, cores), core, operands, specs, outs, []
    )
    return result[0], result[1], list(result[2:])


def before_self_kernel(cores, core, *refs):
    refs = list(refs)
    grads, refs = refs[:cores], refs[cores:]
    queries, refs = refs[:cores], refs[cores:]
    outputs, refs = refs[:cores], refs[cores:]
    d_cross, first, scale, kept = refs[:4]
    sent, refs = refs[4 : 3 + cores], refs[3 + cores :]
    d_attended, d_tokens = refs[:cores], refs[cores]
    total = d_cross[...]
    for value, weight in zip(grads, queries):
        total = total + dot_nt(value[...], weight[0])
    total = norm_back(first[...], scale[...], total)
    d_tokens[...] = total
    low = total.astype(bf16)
    for result, weight in zip(d_attended, outputs):
        result[...] = dot_nt(low, weight[0]).astype(bf16)
    width = kept.shape[1]
    for k, result in enumerate([kept] + sent):
        owner = lax.rem(core[0] + cores - k, cores)
        part = pl.ds(pl.multiple_of(owner * width, width), width)
        result[...] = d_tokens[:, part].astype(result.dtype)


def before_self(core, grads, grads_others, queries, outputs, d_cross, first, scale):
    cores, heads, width = outputs.shape
    rows = first.shape[0]
    operands = [grads] + list(grads_others) + [queries] * cores + [outputs] * cores
    operands += [d_cross, first, scale]
    specs = [at_core(cores, rows, heads)] + [None] * (cores - 1)
    specs += down_from_core(cores, queries.shape[1:]) + down_from_core(cores, outputs.shape[1:])
    specs += [None] * 3
    shape = jax.ShapeDtypeStruct
    outs = [shape((rows, width // cores), f32)] + [shape((rows, width // cores), bf16)] * (cores - 1)
    outs += [shape((rows, heads), bf16)] * cores
    result = one_step(
        functools.partial(before_self_kernel, cores), core, operands, specs, outs,
        [pltpu.VMEM((rows, width), f32)],
    )
    return list(result[:cores]), list(result[cores:])


def beside_kernel(core, *refs):
    which = pl.program_id(0)
    for k, part in enumerate(refs[:-1]):

        @pl.when(which == k)
        def _(part=part):
            refs[-1][...] = part[...].astype(f32)


def beside(core, parts):
    rows, width = parts[0].shape
    cores = len(parts)
    count = 1

    def part_spec(k):
        def place(which, block, core):
            return (jnp.where(which == k, block, jnp.where(which < k, 0, count - 1)), 0)

        return pl.BlockSpec((rows // count, width), place)

    return pl.pallas_call(
        beside_kernel,
        out_shape=jax.ShapeDtypeStruct((rows, cores * width), f32),
        grid_spec=pltpu.PrefetchScalarGridSpec(
            num_scalar_prefetch=1,
            grid=(cores, count),
            in_specs=[part_spec(k) for k in range(cores)],
            out_specs=pl.BlockSpec(
                (rows // count, width),
                lambda which, block, core: (block, lax.rem(core[0] + cores - which, cores)),
            ),
        ),
    )(core, *parts)


def add_kernel(count, each, cut, *refs):
    for i in range(count):
        total = refs[i * each][...].astype(f32)
        for ref in refs[i * each + 1 : i * each + each]:
            total = total + ref[...].astype(f32)
        if cut is None:
            refs[count * each + i][...] = total.astype(bf16)
        else:
            refs[each][...] = total[:cut].astype(bf16)
            refs[each + 1][...] = total[cut:]


def add_up(lists, cut=None):
    each = len(lists[0])
    shape = jax.ShapeDtypeStruct
    outs = [shape(parts[0].shape, bf16) for parts in lists]
    if cut is not None:
        rows, width = lists[0][0].shape
        outs = [shape((cut, width), bf16), shape((rows - cut, width), f32)]
    return pl.pallas_call(
        functools.partial(add_kernel, len(lists), each, cut),
        out_shape=tuple(outs),
        compiler_params=pltpu.CompilerParams(vmem_limit_bytes=60 << 20),
    )(*[part for parts in lists for part in parts])


SMALL = 32


def pack_kernel(count, *refs):
    parts, refs = refs[:count], refs[count:]
    keys, values, biases, out = refs
    rows = parts[0].shape[0]
    total = parts[0][...].astype(f32)
    for part in parts[1:]:
        total = total + part[...].astype(f32)
    out[:rows, :] = total.astype(bf16)
    zero = jnp.zeros((SMALL, out.shape[1] - 2 * keys.shape[1]), f32)
    beside_ = [keys[...], values[...]] + ([zero] if zero.shape[1] else [])
    line = lax.broadcasted_iota(jnp.int32, (SMALL, out.shape[1]), 0)
    rest = jnp.where(line == SMALL - 2, biases[0:1], biases[1:2])
    small = jnp.where(line < SMALL - 2, jnp.concatenate(beside_, axis=1), rest)
    out[rows:, :] = small.astype(bf16)


def pack(parts, keys, values, biases):
    rows, width = parts[0].shape
    return pl.pallas_call(
        functools.partial(pack_kernel, len(parts)),
        out_shape=jax.ShapeDtypeStruct((rows + SMALL, width), bf16),
    )(*parts, keys, values, biases)


def gather_kernel(count, rows, last, place, *refs):
    parts, refs = refs[:count], refs[count:]
    total = parts[0][rows:, :].astype(f32)
    for part in parts[1:]:
        total = total + part[rows:, :].astype(f32)
    if last is None:
        (out,) = refs
        joined = out
        out[count * rows :, :] = total.astype(bf16)
    else:
        keys, values, down, down_bias, up, up_bias, joined = refs
        prefix, cols = keys.shape
        keys[...] = total[:prefix, :cols]
        values[...] = total[:prefix, cols : 2 * cols]
        up_bias[...] = total[SMALL - 2 : SMALL - 1]
        down_bias[...] = total[SMALL - 1 : SMALL, : down_bias.shape[1]]
    for k, part in enumerate(parts):
        owner = jnp.bitwise_xor(place[0], k)
        joined[pl.ds(pl.multiple_of(owner * rows, 16), rows), :] = part[:rows, :]
    if last is not None:
        up[...] = joined[: up.shape[0], :].astype(f32)
        down[...] = joined[up.shape[0] :, :].astype(f32).T


def gather_rows(place, parts, last):
    count = len(parts)
    length, width = parts[0].shape
    rows = length - SMALL
    shape = jax.ShapeDtypeStruct
    if last is None:
        outs, scratch = [shape((count * rows + SMALL, width), bf16)], []
    else:
        prefix, cols, adapt = last
        outs = [
            shape((prefix, cols), f32),
            shape((prefix, cols), f32),
            shape((width, adapt), f32),
            shape((1, adapt), f32),
            shape((adapt, width), f32),
            shape((1, width), f32),
        ]
        scratch = [pltpu.VMEM((count * rows, width), bf16)]
    return one_step(
        functools.partial(gather_kernel, count, rows, last),
        place,
        parts,
        [None] * count,
        outs,
        scratch,
    )


def stack_kernel(cores, core, *refs):
    out = refs[-1]
    rows = refs[0].shape[0]
    for k, part in enumerate(refs[:-1]):
        owner = lax.rem(core[0] + cores - k, cores)
        out[pl.ds(pl.multiple_of(owner * rows, 16), rows), :] = part[...].astype(out.dtype)


def stacked(core, parts):
    rows, width = parts[0].shape
    cores = len(parts)
    out = jax.ShapeDtypeStruct((cores * rows, width), bf16)
    return one_step(
        functools.partial(stack_kernel, cores), core, list(parts), [None] * cores, [out], []
    )[0]


def sum_kernel(places, *refs):
    out = refs[-1]
    for row in range(0, out.shape[0], 128):
        total = jnp.zeros((128, out.shape[1]), f32)
        for ref, place in zip(refs[:-1], places):
            if place <= row < place + ref.shape[0]:
                total = total + ref[row - place : row - place + 128, :].astype(f32)
        out[row : row + 128, :] = total.astype(bf16)


def sum_of(wholes, shorter):
    parts = list(wholes) + [part for part, _ in shorter]
    places = [0] * len(wholes) + [place for _, place in shorter]
    return pl.pallas_call(
        functools.partial(sum_kernel, tuple(places)),
        out_shape=jax.ShapeDtypeStruct(wholes[0].shape, bf16),
        compiler_params=pltpu.CompilerParams(vmem_limit_bytes=60 << 20),
    )(*parts)


def product(left, right):
    return jnp.dot(left, right, preferred_element_type=f32)


def turn(value, distance):
    size = lax.axis_size("head")
    return lax.ppermute(value, "head", [(i, (i + distance) % size) for i in range(size)])


def others(value):
    return [turn(value, k) for k in range(1, lax.axis_size("head"))]


def in_order(parts, axis):
    size = len(parts)
    core = lax.axis_index("head")
    if size == 2:
        first, second = parts
        return jnp.where(
            core == 0,
            jnp.concatenate([first, second], axis=axis),
            jnp.concatenate([second, first], axis=axis),
        )
    ring = jnp.concatenate([parts[-k % size] for k in range(size)] * 2, axis=axis)
    length = parts[0].shape[axis]
    return lax.dynamic_slice_in_dim(ring, (size - core) % size * length, size * length, axis)


def shift(value, distance):
    devices = range(lax.axis_size("seq"))
    return lax.ppermute(value, "seq", [(i, i + distance) for i in devices if i + distance in devices])


def after(value, *first):
    return lax.optimization_barrier((value, first))[0]


class Ring:
    def __init__(self, size, step):
        self.size, self.step = size, step
        self.place = lax.axis_index("seq") // step % size

    def exchange(self, values):
        pairs = [[(i, i ^ k * self.step) for i in range(lax.axis_size("seq"))] for k in range(self.size)]
        return [lax.ppermute(values[k], "seq", pairs[k]) for k in range(1, self.size)]

    def cut(self, value, k):
        length = value.shape[0] // self.size
        return lax.dynamic_slice_in_dim(value, (self.place ^ k) * length, length, 0)

    def scatter(self, value):
        return self.exchange([self.cut(value, k) for k in range(self.size)])


def on_device(
    tokens,
    memory,
    cotangent,
    tgt_lengths,
    mem_lengths,
    self_query,
    self_key,
    self_value,
    self_output,
    cross_query,
    cross_key,
    cross_value,
    cross_output,
    hidden_in,
    hidden_out,
    prefix_keys,
    prefix_values,
    adapter_down,
    adapter_down_bias,
    adapter_up,
    adapter_up_bias,
):
    rows, width = tokens.shape
    cols = self_query.shape[1]
    prefix = prefix_keys.shape[0]
    shards = lax.axis_size("seq")
    position = lax.axis_index("seq")
    core = lax.axis_index("head")
    cores = lax.axis_size("head")
    total = rows * shards
    core_index = jnp.reshape(core, (1,)).astype(jnp.int32)

    def part_of(value, owner, axis=0):
        length = value.shape[axis] // cores
        return lax.dynamic_slice_in_dim(value, owner % cores * length, length, axis)

    def mine(value, axis=0):
        return part_of(value, core, axis)

    def dealt(parts):
        return [parts[0]] + [turn(parts[k], -k) for k in range(1, cores)]

    def over_cores(parts):
        arrived = [part.astype(f32) for part in dealt(parts)]
        return sum(arrived[1:], arrived[0])

    self_far = min(max(-(-(SEQ_MAX - rows) // 128) * 128, 0), rows)
    cross_far = min(max(-(-(SEQ_MAX + DRIFT - rows) // 128) * 128, 0), rows)
    self_base = rows + self_far
    far_rows = 2 * cross_far
    at = jnp.stack([position * rows, core]).astype(jnp.int32)
    base = 3 * rows + PAD
    far_spans = lambda at: (
        (at + rows + cross_far, at, at + cross_far),
        (at + cross_far - 2 * rows, at + cross_far, at + far_rows),
    )
    own_seen, halo_seen, main_seen, far_seen, here_seen, around_seen = see(
        (
            Span(((0, 0, rows),)),
            Span(((self_base, 0, self_base),)),
            Span(((rows, 0, 3 * rows),), False),
            Span(far_spans(0), False),
            Span(((0, 0, rows),), False),
            Span(((rows, 0, rows), (rows, 2 * rows, 3 * rows)) + far_spans(base), False),
        ),
        total,
        rows,
        tgt_lengths,
        mem_lengths,
        at,
    )

    tokens_cols = mine(tokens, 1)
    memory_cols = mine(after(memory, tokens_cols), 1)
    tokens_end = tokens_cols[rows - self_far :]
    token_near = shift(tokens_cols, 1)
    token_far = shift(tokens_end, 2)
    memory_after = shift(memory_cols, -1)
    down_biases = [adapter_down_bias] + others(adapter_down_bias)

    prefix_pad = ((0, 32 - prefix), (0, 0))
    prefix_rows = (
        jnp.pad(prefix_keys.astype(bf16), prefix_pad),
        jnp.pad(prefix_values.astype(bf16), prefix_pad),
        prefix,
    )

    query = (product(tokens, self_query) * (0.125 * LOG2E)).astype(bf16)

    own_keys = product(tokens, self_key).astype(bf16)
    own_values = product(tokens, self_value).astype(bf16)

    def all_cores(value, *first):
        return lax.all_gather(after(value, *first), "head", axis=0)

    self_outputs = all_cores(self_output, query)
    cross_queries = all_cores(cross_query, query)
    arrived = (token_near, token_far)
    memory_keys = product(memory, cross_key).astype(bf16)
    memory_values = product(memory, cross_value).astype(bf16)
    *state, own_keys, own_values = attend(
        query, [(own_keys, own_values)], (self_key, self_value), *own_seen, prefix_rows, last=False
    )
    arrived = (token_near, token_far, memory_after)
    ready = (state, memory_keys, memory_values)
    arrived, ready = lax.optimization_barrier((arrived, ready))
    token_near, token_far, memory_after = arrived
    state, memory_keys, memory_values = ready

    token_near = [token_near] + others(token_near)
    token_far = [token_far] + others(token_far)
    memory_after = [memory_after] + others(after(memory_after, token_near, token_far))
    memory_before = shift(after(memory_cols, token_near, token_far), 1)
    attended, self_lse, halo_keys, halo_values = attend(
        query,
        [Rows(token_far, self_far), Rows(token_near, rows)],
        (self_key, self_value),
        *halo_seen,
        state=state,
    )

    def to_rows(value):
        return [turn(part_of(value, core + k), k) for k in range(1, cores)]

    def to_heads(parts):
        parts = [parts[0]] + [turn(parts[k], -k) for k in range(1, cores)]
        return in_order([parts[-k % cores] for k in range(cores)], 0)

    cross_outputs = all_cores(cross_output, state)
    hidden_ins = all_cores(hidden_in, state)
    hidden_outs = all_cores(hidden_out, state)
    downs = all_cores(after(adapter_down, state).astype(bf16))
    ups = all_cores(after(adapter_up, state).astype(bf16))
    attended_rows = to_rows(attended)
    attended_rows, memory_before, memory_after = lax.optimization_barrier(
        (attended_rows, memory_before, memory_after)
    )
    memory_near = [[memory_before] + others(memory_before), memory_after]
    memory_far = (
        shift(after(memory_cols[rows - cross_far :], memory_near), 2),
        shift(after(memory_cols[:cross_far], memory_near), -2),
    )
    first, first_scale, cross_q = after_self(
        core_index, attended, attended_rows, self_outputs, cross_queries, tokens
    )

    cross_q = to_heads(cross_q)
    *state, main_keys, main_values = attend(
        cross_q,
        [Rows(memory_near[0], rows), (memory_keys, memory_values), Rows(memory_near[1], rows)],
        (cross_key, cross_value),
        *main_seen,
        last=False,
    )
    state, memory_far = lax.optimization_barrier((state, memory_far))
    memory_far = [Rows([part] + others(part), cross_far) for part in memory_far]
    crossed, cross_lse, far_keys, far_values = attend(
        cross_q, memory_far, (cross_key, cross_value), *far_seen, state=state
    )

    (
        outputs_rows,
        d_cross,
        d_crossed,
        adapter_grads,
    ) = feed_forward(
        core_index,
        crossed,
        to_rows(crossed),
        cross_outputs,
        first,
        cotangent,
        downs,
        down_biases,
        ups,
        adapter_up_bias,
        hidden_ins,
        hidden_outs,
    )
    d_crossed = to_heads(d_crossed)
    adapter_grads = dealt(after(adapter_grads, d_crossed))
    outputs_other = others(after(outputs_rows, d_crossed))
    ups_count = adapter_up.shape[0]
    staged = shards >= 4 and shards & (shards - 1) == 0 and 2 * ups_count % (16 * shards) == 0
    if staged:
        plane, column = Ring(4, 1), Ring(shards // 4, 4)

    adapter_grads, bias_grads = add_up([adapter_grads], 2 * ups_count)
    adapter_arrived = []
    if staged:
        adapter_kept = plane.cut(adapter_grads, 0)
        adapter_arrived = plane.scatter(adapter_grads)
        d_crossed = after(d_crossed, adapter_kept)

    cross_weights = (cross_key, cross_value)
    around_grads, query_state = attend_back(
        cross_q,
        d_crossed,
        crossed,
        [(main_keys, main_values, base), (far_keys, far_values, far_rows + PAD)],
        cross_weights,
        *around_seen,
        cross_lse,
        [(0, rows), (2 * rows, rows), (base, cross_far), (base + cross_far, cross_far)],
        cores,
    )
    around_grads, query_state, adapter_arrived, outputs_other = lax.optimization_barrier(
        (around_grads, query_state, adapter_arrived, outputs_other)
    )
    around_parts = [dealt(part) for part in around_grads]
    if staged:
        (adapter_grads,) = add_up([[adapter_kept] + adapter_arrived])
        around_parts = after(around_parts, adapter_grads)
    memory_low = add_up(around_parts)
    memory_arrived = [shift(memory_low[i], distance) for i, distance in enumerate((-1, 1, -2, 2))]
    adapter_arrived = []
    if staged:
        adapter_kept = column.cut(adapter_grads, 0)
        adapter_arrived = column.scatter(after(adapter_grads, memory_low))
        query_state = after(query_state, adapter_kept)
    query_state = after(query_state, memory_low)
    (memory_own,), cross_q_grad = attend_back(
        cross_q,
        d_crossed,
        crossed,
        [(memory_keys, memory_values, rows)],
        cross_weights,
        *here_seen,
        cross_lse,
        [(0, rows)],
        cores,
        state=query_state,
        final=True,
        pad=PAD,
    )
    cross_q_grad, memory_own, memory_near, adapter_arrived = lax.optimization_barrier(
        (cross_q_grad, memory_own, memory_arrived[:2], adapter_arrived)
    )
    grads_rows = to_rows(cross_q_grad)
    memory_own = dealt(after(memory_own, grads_rows))
    d_tokens, d_attended = before_self(
        core_index, cross_q_grad, grads_rows, cross_queries, self_outputs, d_cross, first,
        first_scale,
    )
    d_attended = to_heads(d_attended)
    d_tokens_cols = to_heads(d_tokens)
    memory_own, d_attended, d_tokens_cols = lax.optimization_barrier(
        (memory_own, d_attended, d_tokens_cols)
    )

    self_weights = (self_key, self_value, self_query)
    halo_grads, prefix_key_grad, prefix_value_grad, query_state = attend_back(
        query,
        d_attended,
        attended,
        [(halo_keys, halo_values, self_base + PAD)],
        self_weights,
        *halo_seen,
        self_lse,
        [(0, self_far), (self_far, rows)],
        cores,
        prefix_rows,
    )
    halo_grads, query_state, memory_far = lax.optimization_barrier(
        (halo_grads, query_state, memory_arrived[2:])
    )
    halo_parts = [dealt(part) for part in halo_grads]
    kept = [adapter_kept] + adapter_arrived if staged else [adapter_grads]
    both = pack(kept, prefix_key_grad, prefix_value_grad, bias_grads)
    halo_low = add_up(after(halo_parts, both))
    halo_arrived = (shift(halo_low[0], -2), shift(halo_low[1], -1))
    memory_own, memory_near, memory_far, outputs_rows, outputs_other = after(
        (memory_own, memory_near, memory_far, outputs_rows, outputs_other), halo_low
    )
    memory_sum = sum_of(
        memory_own + list(memory_near), [(memory_far[0], rows - cross_far), (memory_far[1], 0)]
    )
    grad_memory = beside(core_index, [memory_sum] + others(memory_sum))
    outputs = stacked(core_index, [outputs_rows] + outputs_other)
    query_state, grad_memory, outputs = lax.optimization_barrier((query_state, grad_memory, outputs))
    both_arrived = []
    if staged:
        both_arrived = column.exchange([after(both, grad_memory)] * column.size)
    ((here_grads,),) = attend_back(
        query,
        d_attended,
        attended,
        [(own_keys, own_values, rows + PAD)],
        self_weights,
        *own_seen,
        self_lse,
        [(0, rows)],
        cores,
        own=0,
        state=query_state,
    )
    here_grads, halo_arrived, both_arrived = lax.optimization_barrier(
        (here_grads, halo_arrived, both_arrived)
    )
    here_sum = over_cores(here_grads)
    if staged:
        place = jnp.reshape(column.place, (1,)).astype(jnp.int32)
        (both,) = gather_rows(place, [both] + both_arrived, None)
        parts = [both] + plane.exchange([both] * plane.size)
    d_tokens_cols = after(d_tokens_cols, both)
    token_sum = (
        d_tokens_cols.astype(f32)
        + here_sum
        + jnp.pad(halo_arrived[0], ((rows - self_far, 0), (0, 0))).astype(f32)
        + halo_arrived[1].astype(f32)
    ).astype(bf16)
    token_other = others(token_sum)
    grad_tokens = beside(core_index, [token_sum] + token_other)
    if staged:
        place = jnp.reshape(plane.place, (1,)).astype(jnp.int32)
    else:
        parts, place = [lax.psum(both, "seq")], core_index * 0
    parts = after(parts, grad_tokens)
    sizes = (prefix, cols, ups_count)
    prefix_k, prefix_v, grad_down, grad_down_bias, grad_up, grad_up_bias = gather_rows(place, parts, sizes)
    return (
        outputs,
        grad_tokens,
        grad_memory,
        prefix_k,
        prefix_v,
        grad_down,
        grad_down_bias[0],
        grad_up,
        grad_up_bias[0],
    )


def solution(mesh):
    in_specs = (
        P("seq", None),
        P("seq", None),
        P("seq", None),
        P(),
        P(),
        P(None, "head"),
        P(None, "head"),
        P(None, "head"),
        P("head", None),
        P(None, "head"),
        P(None, "head"),
        P(None, "head"),
        P("head", None),
        P(None, "head"),
        P("head", None),
        P(None, "head"),
        P(None, "head"),
        P(None, "head"),
        P("head"),
        P("head", None),
        P(),
    )
    out_specs = (
        P("seq", None),
        P("seq", None),
        P("seq", None),
        P(None, "head"),
        P(None, "head"),
        P(None, "head"),
        P("head"),
        P("head", None),
        P(),
    )
    return jax.shard_map(
        on_device, mesh=mesh, in_specs=in_specs, out_specs=out_specs, check_vma=False
    )
```
